128 devices in a mesh: shot: 8 (over z, y_lo), rcv: 16 (over y_hi, x, core).
Axes of the slice: x: 4, y: 4 (y_hi: 2, y_lo: 2; y = y_hi * 2 + y_lo), z: 4, core: 2. Of those that a mesh axis runs over, the one named last changes fastest.
Arguments:
- traces: bfloat16 [768, 768, 512], P('shot', 'rcv'), may hold values from -6 to 6
- source_weight: float32 [2, 256, 768], P(None, ('shot', 'rcv')), may hold values from -0.15625 to 0.15625
Outputs:
- multiples: bfloat16 [768, 768, 512], P('shot', 'rcv')
The draws below stay inside these ranges and needn't reach their ends.
All inputs are finite; a program needn't handle non-finite values.
Results may differ from the reference program's by a relative error of at most 0.0092.
Values may be sent and summed in bfloat16 or wider, within the bound.
A program may use at most 128 MiB of HBM per device.

```python
import math
import jax
import jax.numpy as jnp
from jax import lax

STATIONS = 768
SAMPLES = 512
FREQS = 256


def block_scale(rng, extent, cuts, smallest, top_value):
    loudness, own = 1.0, jax.random.fold_in(rng, 6)
    for dim, parts in cuts:
        heights = jnp.exp(jax.random.uniform(jax.random.fold_in(own, dim), (parts,), jnp.float32, smallest / len(cuts), top_value / len(cuts)))
        loudness = loudness * jnp.repeat(heights, extent[dim] // parts).reshape([-1 if axis == dim else 1 for axis in range(len(extent))])
    return loudness


def bell_draw(stream_key, dims, spread, bound, shards=(), kind=jnp.bfloat16):
    array = jax.random.normal(stream_key, dims, jnp.float32) * spread
    if len(shards) > 0:
        array = block_scale(stream_key, dims, shards, -0.22, 0.18) * array
    return jnp.clip(array, min=-bound, max=bound).astype(kind)


def setup_inputs(seed: int = 0) -> dict:
    arg_keys = jax.random.split(jax.random.key(seed), 3)
    return {
        "traces": bell_draw(arg_keys[0], (STATIONS, STATIONS, SAMPLES), 1.0, 6.0, ((0, 8), (1, 16))),
        "source_weight": bell_draw(arg_keys[1], (2, FREQS, STATIONS), (2 * STATIONS) ** -0.5, 0.15625, ((1, 128),), jnp.float32),
    }


def dft_basis(count_freq, count_time):
    temporal_pitch = jnp.arange(count_freq, dtype=jnp.int32)
    moments = jnp.arange(count_time, dtype=jnp.int32)
    phase = ((temporal_pitch[:, None] * moments[None, :]) % count_time).astype(jnp.float32) * (2.0 * math.pi / count_time)
    stacked = jnp.stack([jnp.cos(phase), -jnp.sin(phase)], axis=1)
    return stacked.reshape(2 * count_freq, count_time).astype(jnp.bfloat16)


def predict_block(slices, weights):
    summed = slices.astype(jnp.float32) + jnp.swapaxes(slices, 2, 3).astype(jnp.float32)
    averaged = (0.5 * summed).astype(jnp.bfloat16)
    average_inphase_part = averaged[:, 0].astype(jnp.float32)
    average_quadrature_part = averaged[:, 1].astype(jnp.float32)
    weight_real = weights[0][:, :, None]
    weight_imag = weights[1][:, :, None]
    emitter_scaled_inphase = (weight_real * average_inphase_part - weight_imag * average_quadrature_part).astype(jnp.bfloat16).astype(jnp.float32)
    emitter_scaled_quadrature = (weight_real * average_quadrature_part + weight_imag * average_inphase_part).astype(jnp.bfloat16).astype(jnp.float32)
    predicted_inphase_part = jnp.einsum("mgq,mqp->mgp", average_inphase_part, emitter_scaled_inphase) - jnp.einsum("mgq,mqp->mgp", average_quadrature_part, emitter_scaled_quadrature)
    predicted_quadrature_part = jnp.einsum("mgq,mqp->mgp", average_inphase_part, emitter_scaled_quadrature) + jnp.einsum("mgq,mqp->mgp", average_quadrature_part, emitter_scaled_inphase)
    return jnp.stack([predicted_inphase_part, predicted_quadrature_part], axis=1).astype(jnp.bfloat16)


def reference(traces, source_weight):
    basis = dft_basis(FREQS, SAMPLES)
    width = math.gcd(FREQS, 16)
    blocks_total = FREQS // width
    flattened = traces.reshape(STATIONS * STATIONS, SAMPLES)

    def step_block(accumulated, position):
        start = (position * (2 * width)).astype(jnp.int32)
        basis_rows = lax.dynamic_slice_in_dim(basis, start, 2 * width, 0)
        spectra = jnp.dot(flattened, basis_rows.T, preferred_element_type=jnp.float32) * (SAMPLES ** -0.5)
        slices = spectra.astype(jnp.bfloat16).reshape(STATIONS, STATIONS, width, 2).transpose(2, 3, 0, 1)
        weights = lax.dynamic_slice_in_dim(source_weight, (position * width).astype(jnp.int32), width, 1)
        predicted = predict_block(slices, weights)
        flat_pred = predicted.transpose(2, 3, 0, 1).reshape(STATIONS * STATIONS, 2 * width)
        return accumulated + jnp.dot(flat_pred, basis_rows, preferred_element_type=jnp.float32), None

    initial = jnp.zeros((STATIONS * STATIONS, SAMPLES), jnp.float32)
    total, _ = lax.scan(step_block, initial, jnp.arange(blocks_total, dtype=jnp.int32))
    return (total * (2.0 / SAMPLES) ** 0.5).astype(jnp.bfloat16).reshape(STATIONS, STATIONS, SAMPLES)
```

```python
import functools
import math

import jax
import jax.numpy as jnp
import numpy as np
from jax import lax
from jax.experimental import pallas as pl
from jax.experimental.pallas import tpu as pltpu
from jax.sharding import PartitionSpec as P

MESH = pl.DeviceIdType.MESH
BF16, F32 = jnp.bfloat16, jnp.float32

STATIONS = 768
SAMPLES = 512
FREQS = 256
SHOTS = 8
RCVS = 16
DEVS = SHOTS * RCVS
HALF = 48
BAND = 16
BANDS = HALF // BAND
LANES = 128
TILES = 3
ROWS_MSG = TILES * BAND


def basis_table():
    freq = np.arange(FREQS)
    phase = ((freq[:, None] * np.arange(SAMPLES)[None, :]) % SAMPLES).astype(np.float32)
    phase = phase * np.float32(2.0 * math.pi / SAMPLES)
    rows = np.stack([np.cos(phase), -np.sin(phase)], axis=1).reshape(2 * FREQS, SAMPLES)
    rows = rows.reshape(DEVS, 4, SAMPLES).transpose(1, 0, 2).reshape(2 * FREQS, SAMPLES)
    return jnp.asarray(rows.astype(jnp.bfloat16))


def lane_of(rows):
    return lax.broadcasted_iota(jnp.int32, (rows, LANES), 1)


def turned(tile, amount):
    amount %= LANES
    return tile if amount == 0 else pltpu.roll(tile, amount, 1)


def peer(step):
    v = (step * 63) % DEVS
    bits = [(v // (1 << b)) % 2 for b in range(7)]
    dx, dy, dz, dc = 2 * bits[0] + bits[5], 2 * bits[1] + bits[2], 2 * bits[6] + bits[4], bits[3]
    shot, rcv = lax.axis_index("shot"), lax.axis_index("rcv")
    x = ((rcv // 2) % 4 + dx) % 4
    y = ((rcv // 8) * 2 + shot % 2 + dy) % 4
    z = (shot // 2 + dz) % 4
    c = (rcv % 2 + dc) % 2
    return z * 2 + y % 2, (y // 2) * 8 + x * 2 + c


def predict_kernel(
    x_hbm, basis, weight, back, xbuf, fbuf, s1, r1, mbuf, abuf, lbuf, pbuf, s2,
    xsem, send_sem, recv_sem,
):
    shot, rcv = lax.axis_index("shot"), lax.axis_index("rcv")
    me = shot * RCVS + rcv

    def greet(step, carry):
        pl.semaphore_signal(
            pltpu.get_barrier_semaphore(), inc=1, device_id=peer(step), device_id_type=MESH
        )
        return carry

    def x_copy(ts):
        band = pl.ds(ts * BAND, BAND)
        return pltpu.make_async_copy(x_hbm.at[:, band], xbuf.at[:, band], xsem.at[ts])

    for ts in range(BANDS):
        x_copy(ts).start()
    lax.fori_loop(1, DEVS, greet, 0)

    def transform(ts):
        def pair(u, carry):
            rhs = []
            for e in range(2):
                s = ts * BAND + 2 * u + e
                first = xbuf[0, s]
                rhs += [first, xbuf[1, s], first[:32]]
            z = lax.dot_general(
                basis[...], jnp.concatenate(rhs, 0), (((1,), (1,)), ((), ())),
                preferred_element_type=F32,
            )
            lane = lane_of(DEVS)
            for e in range(2):
                zq = [
                    turned(z[q * DEVS : (q + 1) * DEVS, e * LANES : (e + 1) * LANES], 96 * q)
                    for q in range(4)
                ]
                for k in range(TILES):
                    tile = jnp.where(lane < 96 - 32 * k, zq[k], zq[k + 1])
                    fbuf[pl.ds(k * BAND + 2 * u + e, DEVS, stride=ROWS_MSG), :] = (
                        tile * SAMPLES ** (-0.5)
                    )
            return carry

        lax.fori_loop(0, BAND // 2, pair, 0)

        def narrow(g, carry):
            rows = fbuf[pl.ds(pl.multiple_of(g * 8 * ROWS_MSG, 8 * ROWS_MSG), 8 * ROWS_MSG), :]
            s1[pl.ds(g * 8, 8), ts] = rows.astype(BF16).reshape(8, TILES, BAND, LANES)
            return carry

        lax.fori_loop(0, DEVS // 8, narrow, 0)

    def send_all(cut_src, cut_dst, n):
        local = pltpu.make_async_copy(cut_src(me), cut_dst(me), recv_sem.at[n])
        local.start()

        def send(step, carry):
            ps, pr = peer(step)
            pltpu.make_async_remote_copy(
                src_ref=cut_src(ps * RCVS + pr),
                dst_ref=cut_dst(me),
                send_sem=send_sem.at[n],
                recv_sem=recv_sem.at[n],
                device_id=(ps, pr),
                device_id_type=MESH,
            ).start()
            return carry

        lax.fori_loop(1, DEVS, send, 0)

    def wait_recv(ref, n):
        pltpu.make_async_copy(ref, ref, recv_sem.at[n]).wait()

    def wait_send(ref, n):
        pltpu.make_async_copy(ref, ref, send_sem.at[n]).wait()

    for ts in range(BANDS):
        x_copy(ts).wait()
        transform(ts)
        if ts == 0:
            pl.semaphore_wait(pltpu.get_barrier_semaphore(), DEVS - 1)
        send_all(
            lambda d, ts=ts: s1.at[d, ts, pl.ds(0, 2)],
            lambda d, ts=ts: r1.at[d, ts, pl.ds(0, 2)],
            ts,
        )
    send_all(lambda d: s1.at[d, :, 2], lambda d: r1.at[d, :, 2], 3)

    lane = lane_of(BAND)

    def matrix_rows(i, ts, h):
        return pl.ds(pl.multiple_of(i * 96 + h * HALF + ts * BAND, BAND), BAND)

    def assemble(f):
        def step(n, carry):
            i, ts = n // BANDS, n % BANDS
            for jh in range(2):
                near, far = [], []
                for jj in range(8):
                    src = i * RCVS + jh * 8 + jj
                    a, b = r1[src, ts, f], r1[src, ts, f + 1]
                    mixed = jnp.where(lane < 64, b, a)
                    near.append(a if f == 0 else mixed)
                    far.append(mixed if f == 0 else b)
                for gl in range(4):
                    g = 4 * f + gl
                    t = [
                        turned((near if gl < 2 else far)[jj], 48 * (jj - g)) for jj in range(8)
                    ]
                    out = (
                        jnp.where(lane < 48, t[0], jnp.where(lane < 96, t[1], t[2])),
                        jnp.where(
                            lane < 64,
                            jnp.where(lane < 16, t[2], t[3]),
                            jnp.where(lane < 112, t[4], t[5]),
                        ),
                        jnp.where(lane < 32, t[5], jnp.where(lane < 80, t[6], t[7])),
                    )
                    rows = matrix_rows(i, ts, gl % 2)
                    for k in range(TILES):
                        mbuf[gl // 2, rows, pl.ds((jh * TILES + k) * LANES, LANES)] = out[k]
            return carry

        lax.fori_loop(0, SHOTS * BANDS, step, 0)

    def average_and_weight(f):
        def block_row(bi, carry):
            here = pl.ds(pl.multiple_of(bi * LANES, LANES), LANES)
            for bj in range(STATIONS // LANES):
                there = pl.ds(bj * LANES, LANES)
                parts = []
                for c in range(2):
                    both = mbuf[c, here, there].astype(F32) + mbuf[c, there, here].T.astype(F32)
                    parts.append((0.5 * both).astype(BF16))
                abuf[pl.ds(pl.multiple_of(STATIONS + bi * LANES, LANES), LANES), there] = parts[0]
                abuf[here, there] = parts[1]
                ar, ai = parts[0].astype(F32), parts[1].astype(F32)
                wr = weight[0, f : f + 1, there]
                wi = weight[1, f : f + 1, there]
                lr, li = wr * ar - wi * ai, wr * ai + wi * ar
                lbuf[here, there] = (-li).astype(BF16)
                lbuf[here, pl.ds(STATIONS + bj * LANES, LANES)] = lr.astype(BF16)
                lbuf[here, pl.ds(2 * STATIONS + bj * LANES, LANES)] = li.astype(BF16)
            return carry

        lax.fori_loop(0, STATIONS // LANES, block_row, 0)

    def multiply():
        def columns(n, carry):
            cols = pl.ds(pl.multiple_of(n * 256, 256), 256)
            rhs = abuf[:, cols]
            for c in range(2):
                lhs = lbuf[:, c * STATIONS : c * STATIONS + 2 * STATIONS]
                pbuf[c, :, cols] = jnp.dot(lhs, rhs, preferred_element_type=F32).astype(BF16)
            return carry

        lax.fori_loop(0, STATIONS // 256, columns, 0)

    def scatter(f):
        def step(n, carry):
            i, ts = n // BANDS, n % BANDS
            for jh in range(2):
                cut = []
                for gl in range(4):
                    rows = matrix_rows(i, ts, gl % 2)
                    p = [
                        pbuf[gl // 2, rows, pl.ds((jh * TILES + k) * LANES, LANES)]
                        for k in range(TILES)
                    ]
                    p01 = jnp.where(lane < 64, p[1], p[0])
                    p12 = jnp.where(lane < 64, p[2], p[1])
                    held = (p[0], p[0], p01, p[1], p[1], p12, p[2], p[2])
                    cut.append([turned(held[jj], 48 * (4 * f + gl - jj)) for jj in range(8)])
                for jj in range(8):
                    dst = i * RCVS + jh * 8 + jj
                    t = [cut[gl][jj] for gl in range(4)]
                    if f == 0:
                        s2[dst, ts, 0] = jnp.where(
                            lane < 48, t[0], jnp.where(lane < 96, t[1], t[2])
                        )
                        s2[dst, ts, 1] = jnp.where(lane < 16, t[2], t[3])
                    else:
                        s2[dst, ts, 1] = jnp.where(
                            lane < 64, s2[dst, ts, 1], jnp.where(lane < 112, t[0], t[1])
                        )
                        s2[dst, ts, 2] = jnp.where(
                            lane < 32, t[1], jnp.where(lane < 80, t[2], t[3])
                        )
            return carry

        lax.fori_loop(0, SHOTS * BANDS, step, 0)

    for ts in range(BANDS):
        wait_recv(r1.at[:, ts, pl.ds(0, 2)], ts)
    assemble(0)
    average_and_weight(0)
    multiply()
    scatter(0)
    send_all(lambda d: s2.at[d, :, 0], lambda d: back.at[d, :, 0], 4)
    wait_recv(r1.at[:, :, 2], 3)
    assemble(1)
    average_and_weight(1)
    multiply()
    scatter(1)
    send_all(lambda d: s2.at[d, :, pl.ds(1, 2)], lambda d: back.at[d, :, pl.ds(1, 2)], 5)

    others = pl.ds(0, DEVS - 1)
    for ts in range(BANDS):
        wait_send(s1.at[others, ts, pl.ds(0, 2)], ts)
    wait_send(s1.at[others, :, 2], 3)
    wait_send(s2.at[others, :, 0], 4)
    wait_send(s2.at[others, :, pl.ds(1, 2)], 5)
    wait_recv(back.at[:, :, 0], 4)
    wait_recv(back.at[:, :, pl.ds(1, 2)], 5)


def series_kernel(block, basis, out, wide, turn):
    def widen(g, carry):
        rows = block[pl.ds(g * 8, 8), 0].astype(F32).reshape(8 * ROWS_MSG, LANES)
        wide[pl.ds(pl.multiple_of(g * 8 * ROWS_MSG, 8 * ROWS_MSG), 8 * ROWS_MSG), :] = rows
        return carry

    lax.fori_loop(0, DEVS // 8, widen, 0)

    def swap(s, carry):
        tiles = [
            wide[pl.ds(k * BAND + s, DEVS, stride=ROWS_MSG), :].T for k in range(TILES)
        ]
        flat = jnp.concatenate(tiles, 0).astype(BF16)
        rows = pl.ds(pl.multiple_of(s * 96, 96), 96)
        for q in range(4):
            turn[rows, q * DEVS : (q + 1) * DEVS] = flat[96 * q : 96 * (q + 1)]
        return carry

    lax.fori_loop(0, BAND, swap, 0)

    def series(m, carry):
        rows = pl.ds(pl.multiple_of(m * 384, 384), 384)
        value = jnp.dot(turn[rows, :], basis[...], preferred_element_type=F32)
        value = (value * (2.0 / SAMPLES) ** 0.5).astype(BF16)
        for s in range(4):
            for h in range(2):
                low = s * 96 + h * HALF
                out[h, m * 4 + s] = value[low : low + HALF]
        return carry

    lax.fori_loop(0, BAND // 4, series, 0)


def on_device(traces, source_weight):
    basis = basis_table()
    halves = traces.reshape(2, HALF, HALF, SAMPLES)
    back = pl.pallas_call(
        predict_kernel,
        name="predict",
        out_shape=jax.ShapeDtypeStruct((DEVS, BANDS, TILES, BAND, LANES), BF16),
        in_specs=[
            pl.BlockSpec(memory_space=pl.ANY),
            pl.BlockSpec(memory_space=pltpu.VMEM),
            pl.BlockSpec(memory_space=pltpu.VMEM),
        ],
        out_specs=pl.BlockSpec(memory_space=pl.ANY),
        scratch_shapes=[
            pltpu.VMEM((2, HALF, HALF, SAMPLES), BF16),
            pltpu.VMEM((DEVS * ROWS_MSG, LANES), F32),
            pltpu.VMEM((DEVS, BANDS, TILES, BAND, LANES), BF16),
            pltpu.VMEM((DEVS, BANDS, TILES, BAND, LANES), BF16),
            pltpu.VMEM((2, STATIONS, STATIONS), BF16),
            pltpu.VMEM((2 * STATIONS, STATIONS), BF16),
            pltpu.VMEM((STATIONS, 3 * STATIONS), BF16),
            pltpu.VMEM((2, STATIONS, STATIONS), BF16),
            pltpu.VMEM((DEVS, BANDS, TILES, BAND, LANES), BF16),
            pltpu.SemaphoreType.DMA((BANDS,)),
            pltpu.SemaphoreType.DMA((6,)),
            pltpu.SemaphoreType.DMA((6,)),
        ],
        compiler_params=pltpu.CompilerParams(
            collective_id=0, has_side_effects=True, vmem_limit_bytes=56 * 1024 * 1024
        ),
    )(halves, basis, source_weight)
    series = pl.pallas_call(
        series_kernel,
        name="series",
        grid=(BANDS,),
        out_shape=jax.ShapeDtypeStruct((2, HALF, HALF, SAMPLES), BF16),
        in_specs=[
            pl.BlockSpec((DEVS, 1, TILES, BAND, LANES), lambda b: (0, b, 0, 0, 0)),
            pl.BlockSpec((2 * FREQS, SAMPLES), lambda b: (0, 0)),
        ],
        out_specs=pl.BlockSpec((2, BAND, HALF, SAMPLES), lambda b: (0, b, 0, 0)),
        scratch_shapes=[
            pltpu.VMEM((DEVS * ROWS_MSG, LANES), F32),
            pltpu.VMEM((BAND * 96, 2 * FREQS), BF16),
        ],
        compiler_params=pltpu.CompilerParams(vmem_limit_bytes=40 * 1024 * 1024),
    )(back, basis)
    return series.reshape(2 * HALF, HALF, SAMPLES)


def solution(mesh):
    placed = (P("shot", "rcv", None), P(None, ("shot", "rcv"), None))
    return jax.shard_map(
        on_device, mesh=mesh, in_specs=placed, out_specs=P("shot", "rcv", None), check_vma=False
    )
```

```python
import functools
import math

import jax
import jax.numpy as jnp
import numpy as np
from jax import lax
from jax.experimental import pallas as pl
from jax.experimental.pallas import tpu as pltpu
from jax.sharding import PartitionSpec as P

MESH = pl.DeviceIdType.MESH
BF16, F32 = jnp.bfloat16, jnp.float32

STATIONS = 768
SAMPLES = 512
FREQS = 256
SHOTS = 8
RCVS = 16
DEVS = SHOTS * RCVS
HALF = 48
BAND = 16
BANDS = HALF // BAND
LANES = 128
TILES = 3
ROWS_MSG = TILES * BAND


def basis_table():
    freq = np.arange(FREQS)
    phase = ((freq[:, None] * np.arange(SAMPLES)[None, :]) % SAMPLES).astype(np.float32)
    phase = phase * np.float32(2.0 * math.pi / SAMPLES)
    rows = np.stack([np.cos(phase), -np.sin(phase)], axis=1).reshape(2 * FREQS, SAMPLES)
    rows = rows.reshape(DEVS, 4, SAMPLES).transpose(1, 0, 2).reshape(2 * FREQS, SAMPLES)
    return jnp.asarray(rows.astype(jnp.bfloat16))


def lane_of(rows):
    return lax.broadcasted_iota(jnp.int32, (rows, LANES), 1)


def turned(tile, amount):
    amount %= LANES
    return tile if amount == 0 else pltpu.roll(tile, amount, 1)


def peers_in_order():
    shot, rcv = lax.axis_index("shot"), lax.axis_index("rcv")
    x, y, z, c = (rcv // 2) % 4, (rcv // 8) * 2 + shot % 2, shot // 2, rcv % 2
    xs = [2 * ((x + d) % 4) for d in range(4)]
    ys = [((y + d) % 4 % 2, (y + d) % 4 // 2 * 8) for d in range(4)]
    zs = [2 * ((z + d) % 4) for d in range(4)]
    cs = [(c + d) % 2 for d in range(2)]
    order = []
    for step in range(1, DEVS):
        v = step * 63 % DEVS
        bit = [(v >> b) & 1 for b in range(7)]
        dx, dy, dz = 2 * bit[0] + bit[5], 2 * bit[1] + bit[2], 2 * bit[6] + bit[4]
        order.append((zs[dz] + ys[dy][0], ys[dy][1] + xs[dx] + cs[bit[3]]))
    return order


def predict_kernel(
    x_hbm, basis, weight, back, xbuf, fbuf, s1, r1, mbuf, abuf, lbuf, pbuf, s2,
    table, xsem, send_sem, recv_sem,
):
    shot, rcv = lax.axis_index("shot"), lax.axis_index("rcv")
    me = shot * RCVS + rcv

    def x_copy(ts):
        band = pl.ds(ts * BAND, BAND)
        return pltpu.make_async_copy(x_hbm.at[:, band], xbuf.at[:, band], xsem.at[ts])

    for ts in range(BANDS):
        x_copy(ts).start()
    for step, (ps, pr) in enumerate(peers_in_order()):
        pl.semaphore_signal(
            pltpu.get_barrier_semaphore(), inc=1, device_id=(ps, pr), device_id_type=MESH
        )
        table[2 * step] = ps
        table[2 * step + 1] = pr

    def transform(ts):
        def pair(u, carry):
            rhs = []
            for e in range(2):
                s = ts * BAND + 2 * u + e
                first = xbuf[0, s]
                rhs += [first, xbuf[1, s], first[:32]]
            z = lax.dot_general(
                basis[...], jnp.concatenate(rhs, 0), (((1,), (1,)), ((), ())),
                preferred_element_type=F32,
            )
            lane = lane_of(DEVS)
            for e in range(2):
                zq = [
                    turned(z[q * DEVS : (q + 1) * DEVS, e * LANES : (e + 1) * LANES], 96 * q)
                    for q in range(4)
                ]
                for k in range(TILES):
                    tile = jnp.where(lane < 96 - 32 * k, zq[k], zq[k + 1])
                    fbuf[pl.ds(k * BAND + 2 * u + e, DEVS, stride=ROWS_MSG), :] = (
                        tile * SAMPLES ** (-0.5)
                    )
            return carry

        lax.fori_loop(0, BAND // 2, pair, 0, unroll=8)

        def narrow(g, carry):
            rows = fbuf[pl.ds(pl.multiple_of(g * 8 * ROWS_MSG, 8 * ROWS_MSG), 8 * ROWS_MSG), :]
            s1[pl.ds(g * 8, 8), ts] = rows.astype(BF16).reshape(8, TILES, BAND, LANES)
            return carry

        lax.fori_loop(0, DEVS // 8, narrow, 0)

    def send_all(cut_src, cut_dst, n):
        local = pltpu.make_async_copy(cut_src(me), cut_dst(me), recv_sem.at[n])
        local.start()

        def send(step, carry):
            ps, pr = table[2 * step], table[2 * step + 1]
            pltpu.make_async_remote_copy(
                src_ref=cut_src(ps * RCVS + pr),
                dst_ref=cut_dst(me),
                send_sem=send_sem.at[n],
                recv_sem=recv_sem.at[n],
                device_id=(ps, pr),
                device_id_type=MESH,
            ).start()
            return carry

        lax.fori_loop(0, DEVS - 1, send, 0)

    def wait_recv(ref, n):
        pltpu.make_async_copy(ref, ref, recv_sem.at[n]).wait()

    def wait_send(ref, n):
        pltpu.make_async_copy(ref, ref, send_sem.at[n]).wait()

    for ts in range(BANDS):
        x_copy(ts).wait()
        transform(ts)
        if ts == 0:
            pl.semaphore_wait(pltpu.get_barrier_semaphore(), DEVS - 1)
        send_all(
            lambda d, ts=ts: s1.at[d, ts, pl.ds(0, 2)],
            lambda d, ts=ts: r1.at[d, ts, pl.ds(0, 2)],
            ts,
        )
    send_all(lambda d: s1.at[d, :, 2], lambda d: r1.at[d, :, 2], 3)

    lane = lane_of(BAND)

    def matrix_rows(i, ts, h):
        return pl.ds(pl.multiple_of(i * 96 + h * HALF + ts * BAND, BAND), BAND)

    def assemble(f):
        def step(n, carry):
            i, ts = n // BANDS, n % BANDS
            for jh in range(2):
                near, far = [], []
                for jj in range(8):
                    src = i * RCVS + jh * 8 + jj
                    a, b = r1[src, ts, f], r1[src, ts, f + 1]
                    mixed = jnp.where(lane < 64, b, a)
                    near.append(a if f == 0 else mixed)
                    far.append(mixed if f == 0 else b)
                for gl in range(4):
                    g = 4 * f + gl
                    t = [
                        turned((near if gl < 2 else far)[jj], 48 * (jj - g)) for jj in range(8)
                    ]
                    out = (
                        jnp.where(lane < 48, t[0], jnp.where(lane < 96, t[1], t[2])),
                        jnp.where(
                            lane < 64,
                            jnp.where(lane < 16, t[2], t[3]),
                            jnp.where(lane < 112, t[4], t[5]),
                        ),
                        jnp.where(lane < 32, t[5], jnp.where(lane < 80, t[6], t[7])),
                    )
                    rows = matrix_rows(i, ts, gl % 2)
                    for k in range(TILES):
                        mbuf[gl // 2, rows, pl.ds((jh * TILES + k) * LANES, LANES)] = out[k]
            return carry

        lax.fori_loop(0, SHOTS * BANDS, step, 0)

    def average_and_weight(f):
        def block_row(bi, carry):
            here = pl.ds(pl.multiple_of(bi * LANES, LANES), LANES)
            for bj in range(STATIONS // LANES):
                there = pl.ds(bj * LANES, LANES)
                parts = []
                for c in range(2):
                    both = mbuf[c, here, there].astype(F32) + mbuf[c, there, here].T.astype(F32)
                    parts.append((0.5 * both).astype(BF16))
                abuf[pl.ds(pl.multiple_of(STATIONS + bi * LANES, LANES), LANES), there] = parts[0]
                abuf[here, there] = parts[1]
                ar, ai = parts[0].astype(F32), parts[1].astype(F32)
                wr = weight[0, f : f + 1, there]
                wi = weight[1, f : f + 1, there]
                lr, li = wr * ar - wi * ai, wr * ai + wi * ar
                lbuf[here, there] = (-li).astype(BF16)
                lbuf[here, pl.ds(STATIONS + bj * LANES, LANES)] = lr.astype(BF16)
                lbuf[here, pl.ds(2 * STATIONS + bj * LANES, LANES)] = li.astype(BF16)
            return carry

        lax.fori_loop(0, STATIONS // LANES, block_row, 0)

    def multiply():
        def columns(n, carry):
            cols = pl.ds(pl.multiple_of(n * 256, 256), 256)
            rhs = abuf[:, cols]
            for c in range(2):
                lhs = lbuf[:, c * STATIONS : c * STATIONS + 2 * STATIONS]
                pbuf[c, :, cols] = jnp.dot(lhs, rhs, preferred_element_type=F32).astype(BF16)
            return carry

        lax.fori_loop(0, STATIONS // 256, columns, 0)

    def scatter(f):
        def step(n, carry):
            i, ts = n // BANDS, n % BANDS
            for jh in range(2):
                cut = []
                for gl in range(4):
                    rows = matrix_rows(i, ts, gl % 2)
                    p = [
                        pbuf[gl // 2, rows, pl.ds((jh * TILES + k) * LANES, LANES)]
                        for k in range(TILES)
                    ]
                    p01 = jnp.where(lane < 64, p[1], p[0])
                    p12 = jnp.where(lane < 64, p[2], p[1])
                    held = (p[0], p[0], p01, p[1], p[1], p12, p[2], p[2])
                    cut.append([turned(held[jj], 48 * (4 * f + gl - jj)) for jj in range(8)])
                for jj in range(8):
                    dst = i * RCVS + jh * 8 + jj
                    t = [cut[gl][jj] for gl in range(4)]
                    if f == 0:
                        s2[dst, ts, 0] = jnp.where(
                            lane < 48, t[0], jnp.where(lane < 96, t[1], t[2])
                        )
                        s2[dst, ts, 1] = jnp.where(lane < 16, t[2], t[3])
                    else:
                        s2[dst, ts, 1] = jnp.where(
                            lane < 64, s2[dst, ts, 1], jnp.where(lane < 112, t[0], t[1])
                        )
                        s2[dst, ts, 2] = jnp.where(
                            lane < 32, t[1], jnp.where(lane < 80, t[2], t[3])
                        )
            return carry

        lax.fori_loop(0, SHOTS * BANDS, step, 0)

    for ts in range(BANDS):
        wait_recv(r1.at[:, ts, pl.ds(0, 2)], ts)
    assemble(0)
    average_and_weight(0)
    multiply()
    scatter(0)
    send_all(lambda d: s2.at[d, :, 0], lambda d: back.at[d, :, 0], 4)
    wait_recv(r1.at[:, :, 2], 3)
    assemble(1)
    average_and_weight(1)
    multiply()
    scatter(1)
    send_all(lambda d: s2.at[d, :, pl.ds(1, 2)], lambda d: back.at[d, :, pl.ds(1, 2)], 5)

    others = pl.ds(0, DEVS - 1)
    for ts in range(BANDS):
        wait_send(s1.at[others, ts, pl.ds(0, 2)], ts)
    wait_send(s1.at[others, :, 2], 3)
    wait_send(s2.at[others, :, 0], 4)
    wait_send(s2.at[others, :, pl.ds(1, 2)], 5)
    wait_recv(back.at[:, :, 0], 4)
    wait_recv(back.at[:, :, pl.ds(1, 2)], 5)


def series_kernel(block, basis, out, wide, turn):
    def widen(g, carry):
        rows = block[pl.ds(g * 8, 8), 0].astype(F32).reshape(8 * ROWS_MSG, LANES)
        wide[pl.ds(pl.multiple_of(g * 8 * ROWS_MSG, 8 * ROWS_MSG), 8 * ROWS_MSG), :] = rows
        return carry

    lax.fori_loop(0, DEVS // 8, widen, 0)

    def swap(s, carry):
        tiles = [
            wide[pl.ds(k * BAND + s, DEVS, stride=ROWS_MSG), :].astype(BF16).T for k in range(TILES)
        ]
        flat = jnp.concatenate(tiles, 0)
        rows = pl.ds(pl.multiple_of(s * 96, 96), 96)
        for q in range(4):
            turn[rows, q * DEVS : (q + 1) * DEVS] = flat[96 * q : 96 * (q + 1)]
        return carry

    lax.fori_loop(0, BAND, swap, 0, unroll=16)

    def series(m, carry):
        rows = pl.ds(pl.multiple_of(m * 384, 384), 384)
        value = jnp.dot(turn[rows, :], basis[...], preferred_element_type=F32)
        value = (value * (2.0 / SAMPLES) ** 0.5).astype(BF16)
        for s in range(4):
            for h in range(2):
                low = s * 96 + h * HALF
                out[h, m * 4 + s] = value[low : low + HALF]
        return carry

    lax.fori_loop(0, BAND // 4, series, 0, unroll=2)


def on_device(traces, source_weight):
    basis = basis_table()
    halves = traces.reshape(2, HALF, HALF, SAMPLES)
    back = pl.pallas_call(
        predict_kernel,
        name="predict",
        out_shape=jax.ShapeDtypeStruct((DEVS, BANDS, TILES, BAND, LANES), BF16),
        in_specs=[
            pl.BlockSpec(memory_space=pl.ANY),
            pl.BlockSpec(memory_space=pltpu.VMEM),
            pl.BlockSpec(memory_space=pltpu.VMEM),
        ],
        out_specs=pl.BlockSpec(memory_space=pl.ANY),
        scratch_shapes=[
            pltpu.VMEM((2, HALF, HALF, SAMPLES), BF16),
            pltpu.VMEM((DEVS * ROWS_MSG, LANES), F32),
            pltpu.VMEM((DEVS, BANDS, TILES, BAND, LANES), BF16),
            pltpu.VMEM((DEVS, BANDS, TILES, BAND, LANES), BF16),
            pltpu.VMEM((2, STATIONS, STATIONS), BF16),
            pltpu.VMEM((2 * STATIONS, STATIONS), BF16),
            pltpu.VMEM((STATIONS, 3 * STATIONS), BF16),
            pltpu.VMEM((2, STATIONS, STATIONS), BF16),
            pltpu.VMEM((DEVS, BANDS, TILES, BAND, LANES), BF16),
            pltpu.SMEM((2 * DEVS,), jnp.int32),
            pltpu.SemaphoreType.DMA((BANDS,)),
            pltpu.SemaphoreType.DMA((6,)),
            pltpu.SemaphoreType.DMA((6,)),
        ],
        compiler_params=pltpu.CompilerParams(
            collective_id=0, has_side_effects=True, vmem_limit_bytes=56 * 1024 * 1024
        ),
    )(halves, basis, source_weight)
    series = pl.pallas_call(
        series_kernel,
        name="series",
        grid=(BANDS,),
        out_shape=jax.ShapeDtypeStruct((2, HALF, HALF, SAMPLES), BF16),
        in_specs=[
            pl.BlockSpec((DEVS, 1, TILES, BAND, LANES), lambda b: (0, b, 0, 0, 0)),
            pl.BlockSpec((2 * FREQS, SAMPLES), lambda b: (0, 0)),
        ],
        out_specs=pl.BlockSpec((2, BAND, HALF, SAMPLES), lambda b: (0, b, 0, 0)),
        scratch_shapes=[
            pltpu.VMEM((DEVS * ROWS_MSG, LANES), F32),
            pltpu.VMEM((BAND * 96, 2 * FREQS), BF16),
        ],
        compiler_params=pltpu.CompilerParams(vmem_limit_bytes=40 * 1024 * 1024),
    )(back, basis)
    return series.reshape(2 * HALF, HALF, SAMPLES)


def solution(mesh):
    placed = (P("shot", "rcv", None), P(None, ("shot", "rcv"), None))
    return jax.shard_map(
        on_device, mesh=mesh, in_specs=placed, out_specs=P("shot", "rcv", None), check_vma=False
    )
```

```python
import functools
import math

import jax
import jax.numpy as jnp
import numpy as np
from jax import lax
from jax.experimental import pallas as pl
from jax.experimental.pallas import tpu as pltpu
from jax.sharding import PartitionSpec as P

MESH = pl.DeviceIdType.MESH
BF16, F32 = jnp.bfloat16, jnp.float32

STATIONS = 768
SAMPLES = 512
FREQS = 256
SHOTS = 8
RCVS = 16
DEVS = SHOTS * RCVS
HALF = 48
BAND = 16
BANDS = HALF // BAND
LANES = 128
TILES = 3
ROWS_MSG = TILES * BAND


def basis_table():
    freq = np.arange(FREQS)
    phase = ((freq[:, None] * np.arange(SAMPLES)[None, :]) % SAMPLES).astype(np.float32)
    phase = phase * np.float32(2.0 * math.pi / SAMPLES)
    rows = np.stack([np.cos(phase), -np.sin(phase)], axis=1).reshape(2 * FREQS, SAMPLES)
    rows = rows.reshape(DEVS, 4, SAMPLES).transpose(1, 0, 2).reshape(2 * FREQS, SAMPLES)
    return jnp.asarray(rows.astype(jnp.bfloat16))


def lane_of(rows):
    return lax.broadcasted_iota(jnp.int32, (rows, LANES), 1)


def turned(tile, amount):
    amount %= LANES
    return tile if amount == 0 else pltpu.roll(tile, amount, 1)


def peers_in_order():
    shot, rcv = lax.axis_index("shot"), lax.axis_index("rcv")
    x, y, z, c = (rcv // 2) % 4, (rcv // 8) * 2 + shot % 2, shot // 2, rcv % 2
    xs = [2 * ((x + d) % 4) for d in range(4)]
    ys = [((y + d) % 4 % 2, (y + d) % 4 // 2 * 8) for d in range(4)]
    zs = [2 * ((z + d) % 4) for d in range(4)]
    cs = [(c + d) % 2 for d in range(2)]
    order = []
    for step in range(1, DEVS):
        v = step * 63 % DEVS
        bit = [(v >> b) & 1 for b in range(7)]
        dx, dy, dz = 2 * bit[0] + bit[5], 2 * bit[1] + bit[2], 2 * bit[6] + bit[4]
        order.append((zs[dz] + ys[dy][0], ys[dy][1] + xs[dx] + cs[bit[3]]))
    return order


def predict_kernel(
    x_hbm, basis, weight, out_hbm, xbuf, fbuf, s1, r1, mbuf, abuf, lbuf, pbuf, s2, back,
    turn, obuf, table, xsem, osem, send_sem, recv_sem,
):
    shot, rcv = lax.axis_index("shot"), lax.axis_index("rcv")
    me = shot * RCVS + rcv

    def x_copy(ts):
        band = pl.ds(ts * BAND, BAND)
        return pltpu.make_async_copy(x_hbm.at[:, band], xbuf.at[:, band], xsem.at[ts])

    for ts in range(BANDS):
        x_copy(ts).start()
    for step, (ps, pr) in enumerate(peers_in_order()):
        pl.semaphore_signal(
            pltpu.get_barrier_semaphore(), inc=1, device_id=(ps, pr), device_id_type=MESH
        )
        table[2 * step] = ps
        table[2 * step + 1] = pr

    def transform(ts):
        def pair(u, carry):
            rhs = []
            for e in range(2):
                s = ts * BAND + 2 * u + e
                first = xbuf[0, s]
                rhs += [first, xbuf[1, s], first[:32]]
            z = lax.dot_general(
                basis[...], jnp.concatenate(rhs, 0), (((1,), (1,)), ((), ())),
                preferred_element_type=F32,
            )
            lane = lane_of(DEVS)
            for e in range(2):
                zq = [
                    turned(z[q * DEVS : (q + 1) * DEVS, e * LANES : (e + 1) * LANES], 96 * q)
                    for q in range(4)
                ]
                for k in range(TILES):
                    tile = jnp.where(lane < 96 - 32 * k, zq[k], zq[k + 1])
                    fbuf[pl.ds(k * BAND + 2 * u + e, DEVS, stride=ROWS_MSG), :] = (
                        tile * SAMPLES ** (-0.5)
                    )
            return carry

        lax.fori_loop(0, BAND // 2, pair, 0, unroll=8)

        def narrow(g, carry):
            rows = fbuf[pl.ds(pl.multiple_of(g * 8 * ROWS_MSG, 8 * ROWS_MSG), 8 * ROWS_MSG), :]
            s1[pl.ds(g * 8, 8), ts] = rows.astype(BF16).reshape(8, TILES, BAND, LANES)
            return carry

        lax.fori_loop(0, DEVS // 8, narrow, 0)

    def send_all(src, dst, n, bands, tiles):
        pltpu.make_async_copy(
            src.at[me, bands, tiles], dst.at[me, bands, tiles], recv_sem.at[n]
        ).start()

        def send(step, carry):
            ps, pr = table[2 * step], table[2 * step + 1]
            pltpu.make_async_remote_copy(
                src_ref=src.at[ps * RCVS + pr, bands, tiles],
                dst_ref=dst.at[me, bands, tiles],
                send_sem=send_sem.at[n],
                recv_sem=recv_sem.at[n],
                device_id=(ps, pr),
                device_id_type=MESH,
            ).start()
            return carry

        lax.fori_loop(0, DEVS - 1, send, 0)

    def wait_recv(dst, n, bands, tiles):
        ref = dst.at[:, bands, tiles]
        pltpu.make_async_copy(ref, ref, recv_sem.at[n]).wait()

    def wait_send(src, n, bands, tiles):
        ref = src.at[pl.ds(0, DEVS - 1), bands, tiles]
        pltpu.make_async_copy(ref, ref, send_sem.at[n]).wait()

    first, later, lead = pl.ds(0, 1), pl.ds(1, BANDS - 1), pl.ds(0, BANDS - 1)
    x_copy(0).wait()
    transform(0)
    pl.semaphore_wait(pltpu.get_barrier_semaphore(), DEVS - 1)
    send_all(s1, r1, 0, first, pl.ds(0, 2))
    for ts in range(1, BANDS):
        x_copy(ts).wait()
        transform(ts)
    send_all(s1, r1, 1, later, pl.ds(0, 2))
    send_all(s1, r1, 2, pl.ds(0, BANDS), pl.ds(2, 1))

    lane = lane_of(BAND)

    def matrix_rows(i, ts, h):
        return pl.ds(pl.multiple_of(i * 96 + h * HALF + ts * BAND, BAND), BAND)

    def assemble(f):
        def step(n, carry):
            i, ts = n // BANDS, n % BANDS
            for jh in range(2):
                near, far = [], []
                for jj in range(8):
                    src = i * RCVS + jh * 8 + jj
                    a, b = r1[src, ts, f], r1[src, ts, f + 1]
                    mixed = jnp.where(lane < 64, b, a)
                    near.append(a if f == 0 else mixed)
                    far.append(mixed if f == 0 else b)
                for gl in range(4):
                    g = 4 * f + gl
                    t = [
                        turned((near if gl < 2 else far)[jj], 48 * (jj - g)) for jj in range(8)
                    ]
                    out = (
                        jnp.where(lane < 48, t[0], jnp.where(lane < 96, t[1], t[2])),
                        jnp.where(
                            lane < 64,
                            jnp.where(lane < 16, t[2], t[3]),
                            jnp.where(lane < 112, t[4], t[5]),
                        ),
                        jnp.where(lane < 32, t[5], jnp.where(lane < 80, t[6], t[7])),
                    )
                    rows = matrix_rows(i, ts, gl % 2)
                    for k in range(TILES):
                        mbuf[gl // 2, rows, pl.ds((jh * TILES + k) * LANES, LANES)] = out[k]
            return carry

        lax.fori_loop(0, SHOTS * BANDS, step, 0)

    def average_and_weight(f):
        def block_row(bi, carry):
            here = pl.ds(pl.multiple_of(bi * LANES, LANES), LANES)
            for bj in range(STATIONS // LANES):
                there = pl.ds(bj * LANES, LANES)
                parts = []
                for c in range(2):
                    both = mbuf[c, here, there].astype(F32) + mbuf[c, there, here].T.astype(F32)
                    parts.append((0.5 * both).astype(BF16))
                abuf[pl.ds(pl.multiple_of(STATIONS + bi * LANES, LANES), LANES), there] = parts[0]
                abuf[here, there] = parts[1]
                ar, ai = parts[0].astype(F32), parts[1].astype(F32)
                wr = weight[0, f : f + 1, there]
                wi = weight[1, f : f + 1, there]
                lr, li = wr * ar - wi * ai, wr * ai + wi * ar
                lbuf[here, there] = (-li).astype(BF16)
                lbuf[here, pl.ds(STATIONS + bj * LANES, LANES)] = lr.astype(BF16)
                lbuf[here, pl.ds(2 * STATIONS + bj * LANES, LANES)] = li.astype(BF16)
            return carry

        lax.fori_loop(0, STATIONS // LANES, block_row, 0)

    def multiply():
        def columns(n, carry):
            cols = pl.ds(pl.multiple_of(n * 256, 256), 256)
            rhs = abuf[:, cols]
            for c in range(2):
                lhs = lbuf[:, c * STATIONS : c * STATIONS + 2 * STATIONS]
                pbuf[c, :, cols] = jnp.dot(lhs, rhs, preferred_element_type=F32).astype(BF16)
            return carry

        lax.fori_loop(0, STATIONS // 256, columns, 0)

    def scatter(f):
        def step(n, carry):
            i, ts = n // BANDS, n % BANDS
            for jh in range(2):
                cut = []
                for gl in range(4):
                    rows = matrix_rows(i, ts, gl % 2)
                    p = [
                        pbuf[gl // 2, rows, pl.ds((jh * TILES + k) * LANES, LANES)]
                        for k in range(TILES)
                    ]
                    p01 = jnp.where(lane < 64, p[1], p[0])
                    p12 = jnp.where(lane < 64, p[2], p[1])
                    held = (p[0], p[0], p01, p[1], p[1], p12, p[2], p[2])
                    cut.append([turned(held[jj], 48 * (4 * f + gl - jj)) for jj in range(8)])
                for jj in range(8):
                    dst = i * RCVS + jh * 8 + jj
                    t = [cut[gl][jj] for gl in range(4)]
                    if f == 0:
                        s2[dst, ts, 0] = jnp.where(
                            lane < 48, t[0], jnp.where(lane < 96, t[1], t[2])
                        )
                        s2[dst, ts, 1] = jnp.where(lane < 16, t[2], t[3])
                    else:
                        s2[dst, ts, 1] = jnp.where(
                            lane < 64, s2[dst, ts, 1], jnp.where(lane < 112, t[0], t[1])
                        )
                        s2[dst, ts, 2] = jnp.where(
                            lane < 32, t[1], jnp.where(lane < 80, t[2], t[3])
                        )
            return carry

        lax.fori_loop(0, SHOTS * BANDS, step, 0)

    def series(ts):
        flat_back = back.reshape(DEVS * BANDS * ROWS_MSG, LANES)

        def swap(row, carry):
            tiles = [
                flat_back[
                    pl.ds((ts * TILES + k) * BAND + row, DEVS, stride=BANDS * ROWS_MSG), :
                ].T
                for k in range(TILES)
            ]
            flat = jnp.concatenate(tiles, 0)
            rows = pl.ds(pl.multiple_of(row * 96, 96), 96)
            for q in range(4):
                turn[rows, q * DEVS : (q + 1) * DEVS] = flat[96 * q : 96 * (q + 1)]
            return carry

        lax.fori_loop(0, BAND, swap, 0, unroll=16)

        def values(m, carry):
            rows = pl.ds(pl.multiple_of(m * 384, 384), 384)
            value = jnp.dot(turn[rows, :], basis[...], preferred_element_type=F32)
            value = (value * (2.0 / SAMPLES) ** 0.5).astype(BF16)
            for s in range(4):
                for h in range(2):
                    low = s * 96 + h * HALF
                    obuf[h, ts * BAND + m * 4 + s] = value[low : low + HALF]
            return carry

        lax.fori_loop(0, BAND // 4, values, 0, unroll=2)
        out_copy(ts).start()

    def out_copy(ts):
        band = pl.ds(ts * BAND, BAND)
        return pltpu.make_async_copy(obuf.at[:, band], out_hbm.at[:, band], osem.at[ts])

    everything = pl.ds(0, BANDS)
    wait_recv(r1, 0, first, pl.ds(0, 2))
    wait_recv(r1, 1, later, pl.ds(0, 2))
    assemble(0)
    average_and_weight(0)
    multiply()
    scatter(0)
    send_all(s2, back, 3, everything, pl.ds(0, 1))
    wait_recv(r1, 2, everything, pl.ds(2, 1))
    assemble(1)
    average_and_weight(1)
    multiply()
    scatter(1)
    send_all(s2, back, 4, lead, pl.ds(1, 2))
    send_all(s2, back, 5, pl.ds(BANDS - 1, 1), pl.ds(1, 2))
    wait_send(s1, 0, first, pl.ds(0, 2))
    wait_send(s1, 1, later, pl.ds(0, 2))
    wait_send(s1, 2, everything, pl.ds(2, 1))
    wait_send(s2, 3, everything, pl.ds(0, 1))
    wait_recv(back, 3, everything, pl.ds(0, 1))
    wait_recv(back, 4, lead, pl.ds(1, 2))
    for ts in range(BANDS - 1):
        series(ts)
    wait_send(s2, 4, lead, pl.ds(1, 2))
    wait_recv(back, 5, pl.ds(BANDS - 1, 1), pl.ds(1, 2))
    series(BANDS - 1)
    wait_send(s2, 5, pl.ds(BANDS - 1, 1), pl.ds(1, 2))
    for ts in range(BANDS):
        out_copy(ts).wait()


def on_device(traces, source_weight):
    basis = basis_table()
    halves = traces.reshape(2, HALF, HALF, SAMPLES)
    series = pl.pallas_call(
        predict_kernel,
        name="predict",
        out_shape=jax.ShapeDtypeStruct((2, HALF, HALF, SAMPLES), BF16),
        in_specs=[
            pl.BlockSpec(memory_space=pl.ANY),
            pl.BlockSpec(memory_space=pltpu.VMEM),
            pl.BlockSpec(memory_space=pltpu.VMEM),
        ],
        out_specs=pl.BlockSpec(memory_space=pl.ANY),
        scratch_shapes=[
            pltpu.VMEM((2, HALF, HALF, SAMPLES), BF16),
            pltpu.VMEM((DEVS * ROWS_MSG, LANES), F32),
            pltpu.VMEM((DEVS, BANDS, TILES, BAND, LANES), BF16),
            pltpu.VMEM((DEVS, BANDS, TILES, BAND, LANES), BF16),
            pltpu.VMEM((2, STATIONS, STATIONS), BF16),
            pltpu.VMEM((2 * STATIONS, STATIONS), BF16),
            pltpu.VMEM((STATIONS, 3 * STATIONS), BF16),
            pltpu.VMEM((2, STATIONS, STATIONS), BF16),
            pltpu.VMEM((DEVS, BANDS, TILES, BAND, LANES), BF16),
            pltpu.VMEM((DEVS, BANDS, TILES, BAND, LANES), BF16),
            pltpu.VMEM((BAND * 96, 2 * FREQS), BF16),
            pltpu.VMEM((2, HALF, HALF, SAMPLES), BF16),
            pltpu.SMEM((2 * DEVS,), jnp.int32),
            pltpu.SemaphoreType.DMA((BANDS,)),
            pltpu.SemaphoreType.DMA((BANDS,)),
            pltpu.SemaphoreType.DMA((6,)),
            pltpu.SemaphoreType.DMA((6,)),
        ],
        compiler_params=pltpu.CompilerParams(
            collective_id=0, has_side_effects=True, vmem_limit_bytes=56 * 1024 * 1024
        ),
    )(halves, basis, source_weight)
    return series.reshape(2 * HALF, HALF, SAMPLES)


def solution(mesh):
    placed = (P("shot", "rcv", None), P(None, ("shot", "rcv"), None))
    return jax.shard_map(
        on_device, mesh=mesh, in_specs=placed, out_specs=P("shot", "rcv", None), check_vma=False
    )
```

```python
import functools
import math

import jax
import jax.numpy as jnp
import numpy as np
from jax import lax
from jax.experimental import pallas as pl
from jax.experimental.pallas import tpu as pltpu
from jax.sharding import PartitionSpec as P

MESH = pl.DeviceIdType.MESH
BF16, F32 = jnp.bfloat16, jnp.float32

STATIONS = 768
SAMPLES = 512
FREQS = 256
SHOTS = 8
RCVS = 16
DEVS = SHOTS * RCVS
HALF = 48
BAND = 16
BANDS = HALF // BAND
LANES = 128
TILES = 3
ROWS_MSG = TILES * BAND


def basis_table():
    freq = np.arange(FREQS)
    phase = ((freq[:, None] * np.arange(SAMPLES)[None, :]) % SAMPLES).astype(np.float32)
    phase = phase * np.float32(2.0 * math.pi / SAMPLES)
    rows = np.stack([np.cos(phase), -np.sin(phase)], axis=1).reshape(2 * FREQS, SAMPLES)
    rows = rows.reshape(DEVS, 4, SAMPLES).transpose(1, 0, 2).reshape(2 * FREQS, SAMPLES)
    return jnp.asarray(rows.astype(jnp.bfloat16))


def lane_of(rows):
    return lax.broadcasted_iota(jnp.int32, (rows, LANES), 1)


def turned(tile, amount):
    amount %= LANES
    return tile if amount == 0 else pltpu.roll(tile, amount, 1)


def peers_in_order():
    shot, rcv = lax.axis_index("shot"), lax.axis_index("rcv")
    x, y, z, c = (rcv // 2) % 4, (rcv // 8) * 2 + shot % 2, shot // 2, rcv % 2
    xs = [2 * ((x + d) % 4) for d in range(4)]
    ys = [((y + d) % 4 % 2, (y + d) % 4 // 2 * 8) for d in range(4)]
    zs = [2 * ((z + d) % 4) for d in range(4)]
    cs = [(c + d) % 2 for d in range(2)]
    order = []
    for step in range(1, DEVS):
        v = step * 63 % DEVS
        bit = [(v >> b) & 1 for b in range(7)]
        dx, dy, dz = 2 * bit[0] + bit[5], 2 * bit[1] + bit[2], 2 * bit[6] + bit[4]
        order.append((zs[dz] + ys[dy][0], ys[dy][1] + xs[dx] + cs[bit[3]]))
    return order


def predict_kernel(
    x_hbm, basis_hbm, weight_hbm, obuf, basis, weight, xbuf, fbuf, s1, r1, mbuf, abuf, lbuf, pbuf, s2, back,
    turn, table, xsem, psem, send_sem, recv_sem,
):
    shot, rcv = lax.axis_index("shot"), lax.axis_index("rcv")
    me = shot * RCVS + rcv

    def x_copy(ts):
        band = pl.ds(ts * BAND, BAND)
        return pltpu.make_async_copy(x_hbm.at[:, band], xbuf.at[:, band], xsem.at[ts])

    basis_copy = pltpu.make_async_copy(basis_hbm, basis, psem.at[0])
    weight_copy = pltpu.make_async_copy(weight_hbm, weight, psem.at[1])
    x_copy(0).start()
    basis_copy.start()
    for ts in range(1, BANDS):
        x_copy(ts).start()
    weight_copy.start()
    for step, (ps, pr) in enumerate(peers_in_order()):
        pl.semaphore_signal(
            pltpu.get_barrier_semaphore(), inc=1, device_id=(ps, pr), device_id_type=MESH
        )
        table[2 * step] = ps
        table[2 * step + 1] = pr

    def transform(ts):
        def pair(u, carry):
            rhs = []
            for e in range(2):
                s = ts * BAND + 2 * u + e
                first = xbuf[0, s]
                rhs += [first, xbuf[1, s], first[:32]]
            z = lax.dot_general(
                basis[...], jnp.concatenate(rhs, 0), (((1,), (1,)), ((), ())),
                preferred_element_type=F32,
            )
            lane = lane_of(DEVS)
            for e in range(2):
                zq = [
                    turned(z[q * DEVS : (q + 1) * DEVS, e * LANES : (e + 1) * LANES], 96 * q)
                    for q in range(4)
                ]
                for k in range(TILES):
                    tile = jnp.where(lane < 96 - 32 * k, zq[k], zq[k + 1])
                    fbuf[pl.ds(k * BAND + 2 * u + e, DEVS, stride=ROWS_MSG), :] = (
                        tile * SAMPLES ** (-0.5)
                    )
            return carry

        lax.fori_loop(0, BAND // 2, pair, 0, unroll=8)

        def narrow(g, carry):
            rows = fbuf[pl.ds(pl.multiple_of(g * 8 * ROWS_MSG, 8 * ROWS_MSG), 8 * ROWS_MSG), :]
            s1[pl.ds(g * 8, 8), ts] = rows.astype(BF16).reshape(8, TILES, BAND, LANES)
            return carry

        lax.fori_loop(0, DEVS // 8, narrow, 0)

    def send_all(src, dst, n, bands, tiles):
        pltpu.make_async_copy(
            src.at[me, bands, tiles], dst.at[me, bands, tiles], recv_sem.at[n]
        ).start()

        def send(step, carry):
            ps, pr = table[2 * step], table[2 * step + 1]
            pltpu.make_async_remote_copy(
                src_ref=src.at[ps * RCVS + pr, bands, tiles],
                dst_ref=dst.at[me, bands, tiles],
                send_sem=send_sem.at[n],
                recv_sem=recv_sem.at[n],
                device_id=(ps, pr),
                device_id_type=MESH,
            ).start()
            return carry

        lax.fori_loop(0, DEVS - 1, send, 0)

    def wait_recv(dst, n, bands, tiles):
        ref = dst.at[:, bands, tiles]
        pltpu.make_async_copy(ref, ref, recv_sem.at[n]).wait()

    def wait_send(src, n, bands, tiles):
        ref = src.at[pl.ds(0, DEVS - 1), bands, tiles]
        pltpu.make_async_copy(ref, ref, send_sem.at[n]).wait()

    first, later, lead = pl.ds(0, 1), pl.ds(1, BANDS - 1), pl.ds(0, BANDS - 1)
    basis_copy.wait()
    x_copy(0).wait()
    transform(0)
    pl.semaphore_wait(pltpu.get_barrier_semaphore(), DEVS - 1)
    send_all(s1, r1, 0, first, pl.ds(0, 2))
    for ts in range(1, BANDS):
        x_copy(ts).wait()
        transform(ts)
    send_all(s1, r1, 1, later, pl.ds(0, 2))
    send_all(s1, r1, 2, pl.ds(0, BANDS), pl.ds(2, 1))

    lane = lane_of(BAND)

    def matrix_rows(i, ts, h):
        return pl.ds(pl.multiple_of(i * 96 + h * HALF + ts * BAND, BAND), BAND)

    def assemble(f):
        def step(n, carry):
            i, ts = n // BANDS, n % BANDS
            for jh in range(2):
                near, far = [], []
                for jj in range(8):
                    src = i * RCVS + jh * 8 + jj
                    a, b = r1[src, ts, f], r1[src, ts, f + 1]
                    mixed = jnp.where(lane < 64, b, a)
                    near.append(a if f == 0 else mixed)
                    far.append(mixed if f == 0 else b)
                for gl in range(4):
                    g = 4 * f + gl
                    t = [
                        turned((near if gl < 2 else far)[jj], 48 * (jj - g)) for jj in range(8)
                    ]
                    out = (
                        jnp.where(lane < 48, t[0], jnp.where(lane < 96, t[1], t[2])),
                        jnp.where(
                            lane < 64,
                            jnp.where(lane < 16, t[2], t[3]),
                            jnp.where(lane < 112, t[4], t[5]),
                        ),
                        jnp.where(lane < 32, t[5], jnp.where(lane < 80, t[6], t[7])),
                    )
                    rows = matrix_rows(i, ts, gl % 2)
                    for k in range(TILES):
                        mbuf[gl // 2, rows, pl.ds((jh * TILES + k) * LANES, LANES)] = out[k]
            return carry

        lax.fori_loop(0, SHOTS * BANDS, step, 0)

    def average_and_weight(f):
        def block_row(bi, carry):
            here = pl.ds(pl.multiple_of(bi * LANES, LANES), LANES)
            for bj in range(STATIONS // LANES):
                there = pl.ds(bj * LANES, LANES)
                parts = []
                for c in range(2):
                    both = mbuf[c, here, there].astype(F32) + mbuf[c, there, here].T.astype(F32)
                    parts.append((0.5 * both).astype(BF16))
                abuf[pl.ds(pl.multiple_of(STATIONS + bi * LANES, LANES), LANES), there] = parts[0]
                abuf[here, there] = parts[1]
                ar, ai = parts[0].astype(F32), parts[1].astype(F32)
                wr = weight[0, f : f + 1, there]
                wi = weight[1, f : f + 1, there]
                lr, li = wr * ar - wi * ai, wr * ai + wi * ar
                lbuf[here, there] = (-li).astype(BF16)
                lbuf[here, pl.ds(STATIONS + bj * LANES, LANES)] = lr.astype(BF16)
                lbuf[here, pl.ds(2 * STATIONS + bj * LANES, LANES)] = li.astype(BF16)
            return carry

        lax.fori_loop(0, STATIONS // LANES, block_row, 0)

    def multiply():
        def columns(n, carry):
            cols = pl.ds(pl.multiple_of(n * 256, 256), 256)
            rhs = abuf[:, cols]
            for c in range(2):
                lhs = lbuf[:, c * STATIONS : c * STATIONS + 2 * STATIONS]
                pbuf[c, :, cols] = jnp.dot(lhs, rhs, preferred_element_type=F32).astype(BF16)
            return carry

        lax.fori_loop(0, STATIONS // 256, columns, 0)

    def scatter(f):
        def step(n, carry):
            i, ts = n // BANDS, n % BANDS
            for jh in range(2):
                cut = []
                for gl in range(4):
                    rows = matrix_rows(i, ts, gl % 2)
                    p = [
                        pbuf[gl // 2, rows, pl.ds((jh * TILES + k) * LANES, LANES)]
                        for k in range(TILES)
                    ]
                    p01 = jnp.where(lane < 64, p[1], p[0])
                    p12 = jnp.where(lane < 64, p[2], p[1])
                    held = (p[0], p[0], p01, p[1], p[1], p12, p[2], p[2])
                    cut.append([turned(held[jj], 48 * (4 * f + gl - jj)) for jj in range(8)])
                for jj in range(8):
                    dst = i * RCVS + jh * 8 + jj
                    t = [cut[gl][jj] for gl in range(4)]
                    if f == 0:
                        s2[dst, ts, 0] = jnp.where(
                            lane < 48, t[0], jnp.where(lane < 96, t[1], t[2])
                        )
                        s2[dst, ts, 1] = jnp.where(lane < 16, t[2], t[3])
                    else:
                        s2[dst, ts, 1] = jnp.where(
                            lane < 64, s2[dst, ts, 1], jnp.where(lane < 112, t[0], t[1])
                        )
                        s2[dst, ts, 2] = jnp.where(
                            lane < 32, t[1], jnp.where(lane < 80, t[2], t[3])
                        )
            return carry

        lax.fori_loop(0, SHOTS * BANDS, step, 0)

    def series(ts):
        flat_back = back.reshape(DEVS * BANDS * ROWS_MSG, LANES)

        for m in range(BAND // 4):
            for row in range(4 * m, 4 * m + 4):
                tiles = [
                    flat_back[
                        pl.ds((ts * TILES + k) * BAND + row, DEVS, stride=BANDS * ROWS_MSG), :
                    ].T
                    for k in range(TILES)
                ]
                flat = jnp.concatenate(tiles, 0)
                for q in range(4):
                    turn[row * 96 : (row + 1) * 96, q * DEVS : (q + 1) * DEVS] = flat[
                        96 * q : 96 * (q + 1)
                    ]
            value = jnp.dot(
                turn[m * 384 : (m + 1) * 384, :], basis[...], preferred_element_type=F32
            )
            value = (value * (2.0 / SAMPLES) ** 0.5).astype(BF16)
            for s in range(4):
                for h in range(2):
                    low = s * 96 + h * HALF
                    obuf[h, ts * BAND + m * 4 + s] = value[low : low + HALF]

    everything = pl.ds(0, BANDS)
    weight_copy.wait()
    wait_recv(r1, 0, first, pl.ds(0, 2))
    wait_recv(r1, 1, later, pl.ds(0, 2))
    assemble(0)
    average_and_weight(0)
    multiply()
    scatter(0)
    send_all(s2, back, 3, everything, pl.ds(0, 1))
    wait_recv(r1, 2, everything, pl.ds(2, 1))
    assemble(1)
    average_and_weight(1)
    multiply()
    scatter(1)
    send_all(s2, back, 4, lead, pl.ds(1, 2))
    send_all(s2, back, 5, pl.ds(BANDS - 1, 1), pl.ds(1, 2))
    wait_send(s1, 0, first, pl.ds(0, 2))
    wait_send(s1, 1, later, pl.ds(0, 2))
    wait_send(s1, 2, everything, pl.ds(2, 1))
    wait_send(s2, 3, everything, pl.ds(0, 1))
    wait_recv(back, 3, everything, pl.ds(0, 1))
    wait_recv(back, 4, lead, pl.ds(1, 2))
    for ts in range(BANDS - 1):
        series(ts)
    wait_send(s2, 4, lead, pl.ds(1, 2))
    wait_recv(back, 5, pl.ds(BANDS - 1, 1), pl.ds(1, 2))
    series(BANDS - 1)
    wait_send(s2, 5, pl.ds(BANDS - 1, 1), pl.ds(1, 2))


def in_hbm(array):
    return pltpu.with_memory_space_constraint(array, pltpu.HBM)


def on_device(traces, source_weight):
    basis = basis_table()
    halves = traces.reshape(2, HALF, HALF, SAMPLES)
    series = pl.pallas_call(
        predict_kernel,
        name="predict",
        out_shape=jax.ShapeDtypeStruct((2, HALF, HALF, SAMPLES), BF16),
        in_specs=[pl.BlockSpec(memory_space=pltpu.HBM)] * 3,
        out_specs=pl.BlockSpec(memory_space=pltpu.VMEM),
        scratch_shapes=[
            pltpu.VMEM((2 * FREQS, SAMPLES), BF16),
            pltpu.VMEM((2, 2, STATIONS), F32),
            pltpu.VMEM((2, HALF, HALF, SAMPLES), BF16),
            pltpu.VMEM((DEVS * ROWS_MSG, LANES), F32),
            pltpu.VMEM((DEVS, BANDS, TILES, BAND, LANES), BF16),
            pltpu.VMEM((DEVS, BANDS, TILES, BAND, LANES), BF16),
            pltpu.VMEM((2, STATIONS, STATIONS), BF16),
            pltpu.VMEM((2 * STATIONS, STATIONS), BF16),
            pltpu.VMEM((STATIONS, 3 * STATIONS), BF16),
            pltpu.VMEM((2, STATIONS, STATIONS), BF16),
            pltpu.VMEM((DEVS, BANDS, TILES, BAND, LANES), BF16),
            pltpu.VMEM((DEVS, BANDS, TILES, BAND, LANES), BF16),
            pltpu.VMEM((BAND * 96, 2 * FREQS), BF16),
            pltpu.SMEM((2 * DEVS,), jnp.int32),
            pltpu.SemaphoreType.DMA((BANDS,)),
            pltpu.SemaphoreType.DMA((2,)),
            pltpu.SemaphoreType.DMA((6,)),
            pltpu.SemaphoreType.DMA((6,)),
        ],
        compiler_params=pltpu.CompilerParams(
            collective_id=0, has_side_effects=True, vmem_limit_bytes=46 * 1024 * 1024
        ),
    )(halves, in_hbm(basis), in_hbm(source_weight))
    return series.reshape(2 * HALF, HALF, SAMPLES)


def solution(mesh):
    placed = (P("shot", "rcv", None), P(None, ("shot", "rcv"), None))
    return jax.shard_map(
        on_device, mesh=mesh, in_specs=placed, out_specs=P("shot", "rcv", None), check_vma=False
    )
```

```python
import functools
import math

import jax
import jax.numpy as jnp
import numpy as np
from jax import lax
from jax.experimental import pallas as pl
from jax.experimental.pallas import tpu as pltpu
from jax.sharding import PartitionSpec as P

MESH = pl.DeviceIdType.MESH
BF16, F32 = jnp.bfloat16, jnp.float32

STATIONS = 768
SAMPLES = 512
FREQS = 256
SHOTS = 8
RCVS = 16
DEVS = SHOTS * RCVS
HALF = 48
BAND = 16
BANDS = HALF // BAND
LANES = 128
TILES = 3
ROWS_MSG = TILES * BAND


STEPS = (
    85, 84, 117, 116, 83, 52, 53, 77, 87, 92, 76, 93, 82, 86, 94, 10, 95, 11, 81, 4, 79, 27, 54,
    99, 119, 34, 80, 5, 118, 35, 55, 98, 78, 26, 46, 121, 44, 120, 45, 122, 47, 123, 14, 89, 13,
    88, 12, 91, 15, 90, 71, 17, 69, 16, 74, 30, 68, 19, 73, 31, 108, 57, 109, 56, 75, 29, 110,
    59, 111, 58, 72, 28, 70, 18, 105, 39, 114, 38, 115, 61, 104, 60, 102, 41, 125, 40, 20, 64,
    124, 50, 103, 51, 21, 65, 127, 43, 113, 36, 63, 106, 112, 37, 23, 67, 126, 42, 22, 66, 62,
    107, 49, 100, 48, 101, 1, 32, 33, 6, 96, 97, 25, 2, 9, 24, 8, 7, 3,
)


def basis_table():
    freq = np.arange(FREQS)
    phase = ((freq[:, None] * np.arange(SAMPLES)[None, :]) % SAMPLES).astype(np.float32)
    phase = phase * np.float32(2.0 * math.pi / SAMPLES)
    rows = np.stack([np.cos(phase), -np.sin(phase)], axis=1).reshape(2 * FREQS, SAMPLES)
    rows = rows.reshape(DEVS, 4, SAMPLES).transpose(1, 0, 2).reshape(2 * FREQS, SAMPLES)
    return jnp.asarray(rows.astype(jnp.bfloat16))


def lane_of(rows):
    return lax.broadcasted_iota(jnp.int32, (rows, LANES), 1)


def turned(tile, amount):
    amount %= LANES
    return tile if amount == 0 else pltpu.roll(tile, amount, 1)


def peers_in_order():
    shot, rcv = lax.axis_index("shot"), lax.axis_index("rcv")
    x, y, z, c = (rcv // 2) % 4, (rcv // 8) * 2 + shot % 2, shot // 2, rcv % 2
    xs = [2 * ((x + d) % 4) for d in range(4)]
    ys = [((y + d) % 4 % 2, (y + d) % 4 // 2 * 8) for d in range(4)]
    zs = [2 * ((z + d) % 4) for d in range(4)]
    cs = [(c + d) % 2 for d in range(2)]
    order = []
    for step in STEPS:
        dx, dy, dz, dc = step // 32, step // 8 % 4, step // 2 % 4, step % 2
        order.append((zs[dz] + ys[dy][0], ys[dy][1] + xs[dx] + cs[dc]))
    return order


def predict_kernel(
    x_hbm, basis_hbm, weight_hbm, obuf, basis, weight, xbuf, fbuf, s1, r1, mbuf, abuf, lbuf, pbuf, s2, back,
    turn, table, xsem, psem, send_sem, recv_sem,
):
    shot, rcv = lax.axis_index("shot"), lax.axis_index("rcv")
    me = shot * RCVS + rcv

    def x_copy(ts):
        band = pl.ds(ts * BAND, BAND)
        return pltpu.make_async_copy(x_hbm.at[:, band], xbuf.at[:, band], xsem.at[ts])

    basis_copy = pltpu.make_async_copy(basis_hbm, basis, psem.at[0])
    weight_copy = pltpu.make_async_copy(weight_hbm, weight, psem.at[1])
    x_copy(0).start()
    basis_copy.start()
    for ts in range(1, BANDS):
        x_copy(ts).start()
    weight_copy.start()
    for step, (ps, pr) in enumerate(peers_in_order()):
        pl.semaphore_signal(
            pltpu.get_barrier_semaphore(), inc=1, device_id=(ps, pr), device_id_type=MESH
        )
        table[2 * step] = ps
        table[2 * step + 1] = pr

    def transform(ts):
        def pair(u, carry):
            rhs = []
            for e in range(2):
                s = ts * BAND + 2 * u + e
                first = xbuf[0, s]
                rhs += [first, xbuf[1, s], first[:32]]
            z = lax.dot_general(
                basis[...], jnp.concatenate(rhs, 0), (((1,), (1,)), ((), ())),
                preferred_element_type=F32,
            )
            lane = lane_of(DEVS)
            for e in range(2):
                zq = [
                    turned(z[q * DEVS : (q + 1) * DEVS, e * LANES : (e + 1) * LANES], 96 * q)
                    for q in range(4)
                ]
                for k in range(TILES):
                    tile = jnp.where(lane < 96 - 32 * k, zq[k], zq[k + 1])
                    fbuf[pl.ds(k * BAND + 2 * u + e, DEVS, stride=ROWS_MSG), :] = (
                        tile * SAMPLES ** (-0.5)
                    )
            return carry

        lax.fori_loop(0, BAND // 2, pair, 0, unroll=8)

        def narrow(g, carry):
            rows = fbuf[pl.ds(pl.multiple_of(g * 8 * ROWS_MSG, 8 * ROWS_MSG), 8 * ROWS_MSG), :]
            s1[pl.ds(g * 8, 8), ts] = rows.astype(BF16).reshape(8, TILES, BAND, LANES)
            return carry

        lax.fori_loop(0, DEVS // 8, narrow, 0)

    def send_all(src, dst, n, bands, tiles):
        pltpu.make_async_copy(
            src.at[me, bands, tiles], dst.at[me, bands, tiles], recv_sem.at[n]
        ).start()

        def send(step, carry):
            ps, pr = table[2 * step], table[2 * step + 1]
            pltpu.make_async_remote_copy(
                src_ref=src.at[ps * RCVS + pr, bands, tiles],
                dst_ref=dst.at[me, bands, tiles],
                send_sem=send_sem.at[n],
                recv_sem=recv_sem.at[n],
                device_id=(ps, pr),
                device_id_type=MESH,
            ).start()
            return carry

        lax.fori_loop(0, DEVS - 1, send, 0)

    def wait_recv(dst, n, bands, tiles):
        ref = dst.at[:, bands, tiles]
        pltpu.make_async_copy(ref, ref, recv_sem.at[n]).wait()

    def wait_send(src, n, bands, tiles):
        ref = src.at[pl.ds(0, DEVS - 1), bands, tiles]
        pltpu.make_async_copy(ref, ref, send_sem.at[n]).wait()

    first, later, lead = pl.ds(0, 1), pl.ds(1, BANDS - 1), pl.ds(0, BANDS - 1)
    basis_copy.wait()
    x_copy(0).wait()
    transform(0)
    pl.semaphore_wait(pltpu.get_barrier_semaphore(), DEVS - 1)
    send_all(s1, r1, 0, first, pl.ds(0, 2))
    for ts in range(1, BANDS):
        x_copy(ts).wait()
        transform(ts)
    send_all(s1, r1, 1, later, pl.ds(0, 2))
    send_all(s1, r1, 2, pl.ds(0, BANDS), pl.ds(2, 1))

    lane = lane_of(BAND)

    def matrix_rows(i, ts, h):
        return pl.ds(pl.multiple_of(i * 96 + h * HALF + ts * BAND, BAND), BAND)

    def assemble(f):
        def step(n, carry):
            i, ts = n // BANDS, n % BANDS
            for jh in range(2):
                near, far = [], []
                for jj in range(8):
                    src = i * RCVS + jh * 8 + jj
                    a, b = r1[src, ts, f], r1[src, ts, f + 1]
                    mixed = jnp.where(lane < 64, b, a)
                    near.append(a if f == 0 else mixed)
                    far.append(mixed if f == 0 else b)
                for gl in range(4):
                    g = 4 * f + gl
                    t = [
                        turned((near if gl < 2 else far)[jj], 48 * (jj - g)) for jj in range(8)
                    ]
                    out = (
                        jnp.where(lane < 48, t[0], jnp.where(lane < 96, t[1], t[2])),
                        jnp.where(
                            lane < 64,
                            jnp.where(lane < 16, t[2], t[3]),
                            jnp.where(lane < 112, t[4], t[5]),
                        ),
                        jnp.where(lane < 32, t[5], jnp.where(lane < 80, t[6], t[7])),
                    )
                    rows = matrix_rows(i, ts, gl % 2)
                    for k in range(TILES):
                        mbuf[gl // 2, rows, pl.ds((jh * TILES + k) * LANES, LANES)] = out[k]
            return carry

        lax.fori_loop(0, SHOTS * BANDS, step, 0, unroll=3)

    def average_and_weight(f):
        def block_row(bi, carry):
            here = pl.ds(pl.multiple_of(bi * LANES, LANES), LANES)
            for bj in range(STATIONS // LANES):
                there = pl.ds(bj * LANES, LANES)
                parts = []
                for c in range(2):
                    both = mbuf[c, here, there].astype(F32) + mbuf[c, there, here].T.astype(F32)
                    parts.append((0.5 * both).astype(BF16))
                abuf[pl.ds(pl.multiple_of(STATIONS + bi * LANES, LANES), LANES), there] = parts[0]
                abuf[here, there] = parts[1]
                ar, ai = parts[0].astype(F32), parts[1].astype(F32)
                wr = weight[0, f : f + 1, there]
                wi = weight[1, f : f + 1, there]
                lr, li = wr * ar - wi * ai, wr * ai + wi * ar
                lbuf[here, there] = (-li).astype(BF16)
                lbuf[here, pl.ds(STATIONS + bj * LANES, LANES)] = lr.astype(BF16)
                lbuf[here, pl.ds(2 * STATIONS + bj * LANES, LANES)] = li.astype(BF16)
            return carry

        lax.fori_loop(0, STATIONS // LANES, block_row, 0, unroll=6)

    def multiply():
        def columns(n, carry):
            cols = pl.ds(pl.multiple_of(n * 256, 256), 256)
            rhs = abuf[:, cols]
            for c in range(2):
                lhs = lbuf[:, c * STATIONS : c * STATIONS + 2 * STATIONS]
                pbuf[c, :, cols] = jnp.dot(lhs, rhs, preferred_element_type=F32).astype(BF16)
            return carry

        lax.fori_loop(0, STATIONS // 256, columns, 0, unroll=3)

    def scatter(f, low, high):
        def step(n, carry):
            i, ts = n % SHOTS, n // SHOTS
            for jh in range(2):
                cut = []
                for gl in range(4):
                    rows = matrix_rows(i, ts, gl % 2)
                    p = [
                        pbuf[gl // 2, rows, pl.ds((jh * TILES + k) * LANES, LANES)]
                        for k in range(TILES)
                    ]
                    p01 = jnp.where(lane < 64, p[1], p[0])
                    p12 = jnp.where(lane < 64, p[2], p[1])
                    held = (p[0], p[0], p01, p[1], p[1], p12, p[2], p[2])
                    cut.append([turned(held[jj], 48 * (4 * f + gl - jj)) for jj in range(8)])
                for jj in range(8):
                    dst = i * RCVS + jh * 8 + jj
                    t = [cut[gl][jj] for gl in range(4)]
                    if f == 0:
                        s2[dst, ts, 0] = jnp.where(
                            lane < 48, t[0], jnp.where(lane < 96, t[1], t[2])
                        )
                        s2[dst, ts, 1] = jnp.where(lane < 16, t[2], t[3])
                    else:
                        s2[dst, ts, 1] = jnp.where(
                            lane < 64, s2[dst, ts, 1], jnp.where(lane < 112, t[0], t[1])
                        )
                        s2[dst, ts, 2] = jnp.where(
                            lane < 32, t[1], jnp.where(lane < 80, t[2], t[3])
                        )
            return carry

        lax.fori_loop(low * SHOTS, high * SHOTS, step, 0, unroll=4)

    def series(ts):
        flat_back = back.reshape(DEVS * BANDS * ROWS_MSG, LANES)

        for m in range(BAND // 4):
            for row in range(4 * m, 4 * m + 4):
                tiles = [
                    flat_back[
                        pl.ds((ts * TILES + k) * BAND + row, DEVS, stride=BANDS * ROWS_MSG), :
                    ].T
                    for k in range(TILES)
                ]
                flat = jnp.concatenate(tiles, 0)
                for q in range(4):
                    turn[row * 96 : (row + 1) * 96, q * DEVS : (q + 1) * DEVS] = flat[
                        96 * q : 96 * (q + 1)
                    ]
            value = jnp.dot(
                turn[m * 384 : (m + 1) * 384, :], basis[...], preferred_element_type=F32
            )
            value = (value * (2.0 / SAMPLES) ** 0.5).astype(BF16)
            for s in range(4):
                for h in range(2):
                    low = s * 96 + h * HALF
                    obuf[h, ts * BAND + m * 4 + s] = value[low : low + HALF]

    everything = pl.ds(0, BANDS)
    weight_copy.wait()
    wait_recv(r1, 0, first, pl.ds(0, 2))
    wait_recv(r1, 1, later, pl.ds(0, 2))
    assemble(0)
    average_and_weight(0)
    multiply()
    scatter(0, 0, BANDS)
    send_all(s2, back, 3, everything, pl.ds(0, 1))
    wait_recv(r1, 2, everything, pl.ds(2, 1))
    assemble(1)
    average_and_weight(1)
    multiply()
    scatter(1, 0, BANDS - 1)
    send_all(s2, back, 4, lead, pl.ds(1, 2))
    scatter(1, BANDS - 1, BANDS)
    send_all(s2, back, 5, pl.ds(BANDS - 1, 1), pl.ds(1, 2))
    wait_send(s1, 0, first, pl.ds(0, 2))
    wait_send(s1, 1, later, pl.ds(0, 2))
    wait_send(s1, 2, everything, pl.ds(2, 1))
    wait_send(s2, 3, everything, pl.ds(0, 1))
    wait_recv(back, 3, everything, pl.ds(0, 1))
    wait_recv(back, 4, lead, pl.ds(1, 2))
    for ts in range(BANDS - 1):
        series(ts)
    wait_send(s2, 4, lead, pl.ds(1, 2))
    wait_recv(back, 5, pl.ds(BANDS - 1, 1), pl.ds(1, 2))
    series(BANDS - 1)
    wait_send(s2, 5, pl.ds(BANDS - 1, 1), pl.ds(1, 2))


def in_hbm(array):
    return pltpu.with_memory_space_constraint(array, pltpu.HBM)


def on_device(traces, source_weight):
    basis = basis_table()
    halves = traces.reshape(2, HALF, HALF, SAMPLES)
    series = pl.pallas_call(
        predict_kernel,
        name="predict",
        out_shape=jax.ShapeDtypeStruct((2, HALF, HALF, SAMPLES), BF16),
        in_specs=[pl.BlockSpec(memory_space=pltpu.HBM)] * 3,
        out_specs=pl.BlockSpec(memory_space=pltpu.VMEM),
        scratch_shapes=[
            pltpu.VMEM((2 * FREQS, SAMPLES), BF16),
            pltpu.VMEM((2, 2, STATIONS), F32),
            pltpu.VMEM((2, HALF, HALF, SAMPLES), BF16),
            pltpu.VMEM((DEVS * ROWS_MSG, LANES), F32),
            pltpu.VMEM((DEVS, BANDS, TILES, BAND, LANES), BF16),
            pltpu.VMEM((DEVS, BANDS, TILES, BAND, LANES), BF16),
            pltpu.VMEM((2, STATIONS, STATIONS), BF16),
            pltpu.VMEM((2 * STATIONS, STATIONS), BF16),
            pltpu.VMEM((STATIONS, 3 * STATIONS), BF16),
            pltpu.VMEM((2, STATIONS, STATIONS), BF16),
            pltpu.VMEM((DEVS, BANDS, TILES, BAND, LANES), BF16),
            pltpu.VMEM((DEVS, BANDS, TILES, BAND, LANES), BF16),
            pltpu.VMEM((BAND * 96, 2 * FREQS), BF16),
            pltpu.SMEM((2 * DEVS,), jnp.int32),
            pltpu.SemaphoreType.DMA((BANDS,)),
            pltpu.SemaphoreType.DMA((2,)),
            pltpu.SemaphoreType.DMA((6,)),
            pltpu.SemaphoreType.DMA((6,)),
        ],
        compiler_params=pltpu.CompilerParams(
            collective_id=0, has_side_effects=True, vmem_limit_bytes=46 * 1024 * 1024
        ),
    )(halves, in_hbm(basis), in_hbm(source_weight))
    return series.reshape(2 * HALF, HALF, SAMPLES)


def solution(mesh):
    placed = (P("shot", "rcv", None), P(None, ("shot", "rcv"), None))
    return jax.shard_map(
        on_device, mesh=mesh, in_specs=placed, out_specs=P("shot", "rcv", None), check_vma=False
    )
```

```python
import functools
import math

import jax
import jax.numpy as jnp
import numpy as np
from jax import lax
from jax.experimental import pallas as pl
from jax.experimental.pallas import tpu as pltpu
from jax.sharding import PartitionSpec as P

MESH = pl.DeviceIdType.MESH
BF16, F32 = jnp.bfloat16, jnp.float32

STATIONS = 768
SAMPLES = 512
FREQS = 256
SHOTS = 8
RCVS = 16
DEVS = SHOTS * RCVS
HALF = 48
BAND = 16
BANDS = HALF // BAND
LANES = 128
TILES = 3
ROWS_MSG = TILES * BAND


STEPS = (
    85, 84, 86, 2, 87, 116, 34, 119, 52, 67, 118, 53, 66, 22, 77, 91, 83, 7, 92, 8, 82, 6, 76,
    25, 93, 9, 117, 32, 1, 124, 40, 125, 41, 21, 65, 108, 24, 69, 17, 68, 16, 37, 113, 36, 112,
    95, 10, 94, 3, 79, 26, 78, 27, 46, 122, 47, 123, 44, 121, 45, 120, 75, 31, 74, 30, 109, 33,
    51, 102, 50, 103, 19, 71, 18, 70, 81, 5, 80, 4, 114, 39, 115, 38, 90, 15, 106, 62, 107, 63,
    60, 105, 20, 64, 54, 99, 55, 98, 61, 104, 59, 110, 58, 111, 29, 72, 28, 73, 42, 127, 23, 35,
    96, 12, 57, 97, 13, 56, 100, 48, 101, 49, 126, 43, 88, 11, 89, 14,
)


def basis_table():
    freq = np.arange(FREQS)
    phase = ((freq[:, None] * np.arange(SAMPLES)[None, :]) % SAMPLES).astype(np.float32)
    phase = phase * np.float32(2.0 * math.pi / SAMPLES)
    rows = np.stack([np.cos(phase), -np.sin(phase)], axis=1).reshape(2 * FREQS, SAMPLES)
    rows = rows.reshape(DEVS, 4, SAMPLES).transpose(1, 0, 2).reshape(2 * FREQS, SAMPLES)
    return jnp.asarray(rows.astype(jnp.bfloat16))


def lane_of(rows):
    return lax.broadcasted_iota(jnp.int32, (rows, LANES), 1)


def turned(tile, amount):
    amount %= LANES
    return tile if amount == 0 else pltpu.roll(tile, amount, 1)


def peers_in_order():
    shot, rcv = lax.axis_index("shot"), lax.axis_index("rcv")
    x, y, z, c = (rcv // 2) % 4, (rcv // 8) * 2 + shot % 2, shot // 2, rcv % 2
    xs = [2 * ((x + d) % 4) for d in range(4)]
    ys = [((y + d) % 4 % 2, (y + d) % 4 // 2 * 8) for d in range(4)]
    zs = [2 * ((z + d) % 4) for d in range(4)]
    cs = [(c + d) % 2 for d in range(2)]
    order = []
    for step in STEPS:
        dx, dy, dz, dc = step // 32, step // 8 % 4, step // 2 % 4, step % 2
        order.append((zs[dz] + ys[dy][0], ys[dy][1] + xs[dx] + cs[dc]))
    return order


def predict_kernel(
    x_hbm, basis_hbm, weight_hbm, obuf, basis, weight, xbuf, fbuf, s1, r1, mbuf, abuf, lbuf, pbuf, s2, back,
    turn, table, xsem, psem, send_sem, recv_sem,
):
    shot, rcv = lax.axis_index("shot"), lax.axis_index("rcv")
    me = shot * RCVS + rcv

    def x_copy(ts):
        band = pl.ds(ts * BAND, BAND)
        return pltpu.make_async_copy(x_hbm.at[:, band], xbuf.at[:, band], xsem.at[ts])

    basis_copy = pltpu.make_async_copy(basis_hbm, basis, psem.at[0])
    weight_copy = pltpu.make_async_copy(weight_hbm, weight, psem.at[1])
    x_copy(0).start()
    basis_copy.start()
    for ts in range(1, BANDS):
        x_copy(ts).start()
    weight_copy.start()
    for step, (ps, pr) in enumerate(peers_in_order()):
        pl.semaphore_signal(
            pltpu.get_barrier_semaphore(), inc=1, device_id=(ps, pr), device_id_type=MESH
        )
        table[2 * step] = ps
        table[2 * step + 1] = pr

    def transform(ts):
        def pair(u, carry):
            rhs = []
            for e in range(2):
                s = ts * BAND + 2 * u + e
                first = xbuf[0, s]
                rhs += [first, xbuf[1, s], first[:32]]
            z = lax.dot_general(
                basis[...], jnp.concatenate(rhs, 0), (((1,), (1,)), ((), ())),
                preferred_element_type=F32,
            )
            lane = lane_of(DEVS)
            for e in range(2):
                zq = [
                    turned(z[q * DEVS : (q + 1) * DEVS, e * LANES : (e + 1) * LANES], 96 * q)
                    for q in range(4)
                ]
                for k in range(TILES):
                    tile = jnp.where(lane < 96 - 32 * k, zq[k], zq[k + 1])
                    fbuf[pl.ds(k * BAND + 2 * u + e, DEVS, stride=ROWS_MSG), :] = (
                        tile * SAMPLES ** (-0.5)
                    )
            return carry

        lax.fori_loop(0, BAND // 2, pair, 0, unroll=8)

        def narrow(g, carry):
            rows = fbuf[pl.ds(pl.multiple_of(g * 8 * ROWS_MSG, 8 * ROWS_MSG), 8 * ROWS_MSG), :]
            s1[pl.ds(g * 8, 8), ts] = rows.astype(BF16).reshape(8, TILES, BAND, LANES)
            return carry

        lax.fori_loop(0, DEVS // 8, narrow, 0)

    def send_all(src, dst, n, bands, tiles):
        pltpu.make_async_copy(
            src.at[me, bands, tiles], dst.at[me, bands, tiles], recv_sem.at[n]
        ).start()

        def send(step, carry):
            ps, pr = table[2 * step], table[2 * step + 1]
            pltpu.make_async_remote_copy(
                src_ref=src.at[ps * RCVS + pr, bands, tiles],
                dst_ref=dst.at[me, bands, tiles],
                send_sem=send_sem.at[n],
                recv_sem=recv_sem.at[n],
                device_id=(ps, pr),
                device_id_type=MESH,
            ).start()
            return carry

        lax.fori_loop(0, DEVS - 1, send, 0)

    def wait_recv(dst, n, bands, tiles):
        ref = dst.at[:, bands, tiles]
        pltpu.make_async_copy(ref, ref, recv_sem.at[n]).wait()

    def wait_send(src, n, bands, tiles):
        ref = src.at[pl.ds(0, DEVS - 1), bands, tiles]
        pltpu.make_async_copy(ref, ref, send_sem.at[n]).wait()

    first, later, lead = pl.ds(0, 1), pl.ds(1, BANDS - 1), pl.ds(0, BANDS - 1)
    basis_copy.wait()
    x_copy(0).wait()
    transform(0)
    pl.semaphore_wait(pltpu.get_barrier_semaphore(), DEVS - 1)
    send_all(s1, r1, 0, first, pl.ds(0, 2))
    for ts in range(1, BANDS):
        x_copy(ts).wait()
        transform(ts)
    send_all(s1, r1, 1, later, pl.ds(0, 2))
    send_all(s1, r1, 2, pl.ds(0, BANDS), pl.ds(2, 1))

    lane = lane_of(BAND)

    def matrix_rows(i, ts, h):
        return pl.ds(pl.multiple_of(i * 96 + h * HALF + ts * BAND, BAND), BAND)

    def assemble(f):
        def step(n, carry):
            i, ts = n // BANDS, n % BANDS
            for jh in range(2):
                near, far = [], []
                for jj in range(8):
                    src = i * RCVS + jh * 8 + jj
                    a, b = r1[src, ts, f], r1[src, ts, f + 1]
                    mixed = jnp.where(lane < 64, b, a)
                    near.append(a if f == 0 else mixed)
                    far.append(mixed if f == 0 else b)
                for gl in range(4):
                    g = 4 * f + gl
                    t = [
                        turned((near if gl < 2 else far)[jj], 48 * (jj - g)) for jj in range(8)
                    ]
                    out = (
                        jnp.where(lane < 48, t[0], jnp.where(lane < 96, t[1], t[2])),
                        jnp.where(
                            lane < 64,
                            jnp.where(lane < 16, t[2], t[3]),
                            jnp.where(lane < 112, t[4], t[5]),
                        ),
                        jnp.where(lane < 32, t[5], jnp.where(lane < 80, t[6], t[7])),
                    )
                    rows = matrix_rows(i, ts, gl % 2)
                    for k in range(TILES):
                        mbuf[gl // 2, rows, pl.ds((jh * TILES + k) * LANES, LANES)] = out[k]
            return carry

        lax.fori_loop(0, SHOTS * BANDS, step, 0, unroll=3)

    def average_and_weight(f):
        def block_row(bi, carry):
            here = pl.ds(pl.multiple_of(bi * LANES, LANES), LANES)
            for bj in range(STATIONS // LANES):
                there = pl.ds(bj * LANES, LANES)
                parts = []
                for c in range(2):
                    both = mbuf[c, here, there].astype(F32) + mbuf[c, there, here].T.astype(F32)
                    parts.append((0.5 * both).astype(BF16))
                abuf[pl.ds(pl.multiple_of(STATIONS + bi * LANES, LANES), LANES), there] = parts[0]
                abuf[here, there] = parts[1]
                ar, ai = parts[0].astype(F32), parts[1].astype(F32)
                wr = weight[0, f : f + 1, there]
                wi = weight[1, f : f + 1, there]
                lr, li = wr * ar - wi * ai, wr * ai + wi * ar
                lbuf[here, there] = (-li).astype(BF16)
                lbuf[here, pl.ds(STATIONS + bj * LANES, LANES)] = lr.astype(BF16)
                lbuf[here, pl.ds(2 * STATIONS + bj * LANES, LANES)] = li.astype(BF16)
            return carry

        lax.fori_loop(0, STATIONS // LANES, block_row, 0, unroll=6)

    def multiply():
        def columns(n, carry):
            cols = pl.ds(pl.multiple_of(n * 256, 256), 256)
            rhs = abuf[:, cols]
            for c in range(2):
                lhs = lbuf[:, c * STATIONS : c * STATIONS + 2 * STATIONS]
                pbuf[c, :, cols] = jnp.dot(lhs, rhs, preferred_element_type=F32).astype(BF16)
            return carry

        lax.fori_loop(0, STATIONS // 256, columns, 0, unroll=3)

    def scatter(f, low, high):
        def step(n, carry):
            i, ts = n % SHOTS, n // SHOTS
            for jh in range(2):
                cut = []
                for gl in range(4):
                    rows = matrix_rows(i, ts, gl % 2)
                    p = [
                        pbuf[gl // 2, rows, pl.ds((jh * TILES + k) * LANES, LANES)]
                        for k in range(TILES)
                    ]
                    p01 = jnp.where(lane < 64, p[1], p[0])
                    p12 = jnp.where(lane < 64, p[2], p[1])
                    held = (p[0], p[0], p01, p[1], p[1], p12, p[2], p[2])
                    cut.append([turned(held[jj], 48 * (4 * f + gl - jj)) for jj in range(8)])
                for jj in range(8):
                    dst = i * RCVS + jh * 8 + jj
                    t = [cut[gl][jj] for gl in range(4)]
                    if f == 0:
                        s2[dst, ts, 0] = jnp.where(
                            lane < 48, t[0], jnp.where(lane < 96, t[1], t[2])
                        )
                        s2[dst, ts, 1] = jnp.where(lane < 16, t[2], t[3])
                    else:
                        s2[dst, ts, 1] = jnp.where(
                            lane < 64, s2[dst, ts, 1], jnp.where(lane < 112, t[0], t[1])
                        )
                        s2[dst, ts, 2] = jnp.where(
                            lane < 32, t[1], jnp.where(lane < 80, t[2], t[3])
                        )
            return carry

        lax.fori_loop(low * SHOTS, high * SHOTS, step, 0, unroll=4)

    def series(ts):
        flat_back = back.reshape(DEVS * BANDS * ROWS_MSG, LANES)

        for m in range(BAND // 4):
            for row in range(4 * m, 4 * m + 4):
                tiles = [
                    flat_back[
                        pl.ds((ts * TILES + k) * BAND + row, DEVS, stride=BANDS * ROWS_MSG), :
                    ].T
                    for k in range(TILES)
                ]
                flat = jnp.concatenate(tiles, 0)
                for q in range(4):
                    turn[row * 96 : (row + 1) * 96, q * DEVS : (q + 1) * DEVS] = flat[
                        96 * q : 96 * (q + 1)
                    ]
            value = jnp.dot(
                turn[m * 384 : (m + 1) * 384, :], basis[...], preferred_element_type=F32
            )
            value = (value * (2.0 / SAMPLES) ** 0.5).astype(BF16)
            for s in range(4):
                for h in range(2):
                    low = s * 96 + h * HALF
                    obuf[h, ts * BAND + m * 4 + s] = value[low : low + HALF]

    everything = pl.ds(0, BANDS)
    weight_copy.wait()
    wait_recv(r1, 0, first, pl.ds(0, 2))
    wait_recv(r1, 1, later, pl.ds(0, 2))
    assemble(0)
    average_and_weight(0)
    multiply()
    scatter(0, 0, BANDS)
    send_all(s2, back, 3, everything, pl.ds(0, 1))
    wait_recv(r1, 2, everything, pl.ds(2, 1))
    assemble(1)
    average_and_weight(1)
    multiply()
    scatter(1, 0, BANDS - 1)
    send_all(s2, back, 4, lead, pl.ds(1, 2))
    scatter(1, BANDS - 1, BANDS)
    send_all(s2, back, 5, pl.ds(BANDS - 1, 1), pl.ds(1, 2))
    wait_send(s1, 0, first, pl.ds(0, 2))
    wait_send(s1, 1, later, pl.ds(0, 2))
    wait_send(s1, 2, everything, pl.ds(2, 1))
    wait_send(s2, 3, everything, pl.ds(0, 1))
    wait_recv(back, 3, everything, pl.ds(0, 1))
    wait_recv(back, 4, lead, pl.ds(1, 2))
    for ts in range(BANDS - 1):
        series(ts)
    wait_send(s2, 4, lead, pl.ds(1, 2))
    wait_recv(back, 5, pl.ds(BANDS - 1, 1), pl.ds(1, 2))
    series(BANDS - 1)
    wait_send(s2, 5, pl.ds(BANDS - 1, 1), pl.ds(1, 2))


def in_hbm(array):
    return pltpu.with_memory_space_constraint(array, pltpu.HBM)


def on_device(traces, source_weight):
    basis = basis_table()
    halves = traces.reshape(2, HALF, HALF, SAMPLES)
    series = pl.pallas_call(
        predict_kernel,
        name="predict",
        out_shape=jax.ShapeDtypeStruct((2, HALF, HALF, SAMPLES), BF16),
        in_specs=[pl.BlockSpec(memory_space=pltpu.HBM)] * 3,
        out_specs=pl.BlockSpec(memory_space=pltpu.VMEM),
        scratch_shapes=[
            pltpu.VMEM((2 * FREQS, SAMPLES), BF16),
            pltpu.VMEM((2, 2, STATIONS), F32),
            pltpu.VMEM((2, HALF, HALF, SAMPLES), BF16),
            pltpu.VMEM((DEVS * ROWS_MSG, LANES), F32),
            pltpu.VMEM((DEVS, BANDS, TILES, BAND, LANES), BF16),
            pltpu.VMEM((DEVS, BANDS, TILES, BAND, LANES), BF16),
            pltpu.VMEM((2, STATIONS, STATIONS), BF16),
            pltpu.VMEM((2 * STATIONS, STATIONS), BF16),
            pltpu.VMEM((STATIONS, 3 * STATIONS), BF16),
            pltpu.VMEM((2, STATIONS, STATIONS), BF16),
            pltpu.VMEM((DEVS, BANDS, TILES, BAND, LANES), BF16),
            pltpu.VMEM((DEVS, BANDS, TILES, BAND, LANES), BF16),
            pltpu.VMEM((BAND * 96, 2 * FREQS), BF16),
            pltpu.SMEM((2 * DEVS,), jnp.int32),
            pltpu.SemaphoreType.DMA((BANDS,)),
            pltpu.SemaphoreType.DMA((2,)),
            pltpu.SemaphoreType.DMA((6,)),
            pltpu.SemaphoreType.DMA((6,)),
        ],
        compiler_params=pltpu.CompilerParams(
            collective_id=0, has_side_effects=True, vmem_limit_bytes=46 * 1024 * 1024
        ),
    )(halves, in_hbm(basis), in_hbm(source_weight))
    return series.reshape(2 * HALF, HALF, SAMPLES)


def solution(mesh):
    placed = (P("shot", "rcv", None), P(None, ("shot", "rcv"), None))
    return jax.shard_map(
        on_device, mesh=mesh, in_specs=placed, out_specs=P("shot", "rcv", None), check_vma=False
    )
```
